32 devices in a mesh: ctx: 16 (over z, y, core), head: 2 (over x).
Axes of the slice: x: 2, y: 2, z: 4, core: 2. Of those that a mesh axis runs over, the one named last changes fastest.
Arguments:
- key_rows: bfloat16 [16384, 2560], P('ctx', 'head'), may hold values from -6 to 6
- value_rows: bfloat16 [16384, 2560], P('ctx', 'head'), may hold values from -6 to 6
- query_rows: bfloat16 [16384, 2560], P('ctx', 'head'), may hold values from -6 to 6
- learn_rates: float32 [4, 16384], P('head', 'ctx'), may hold values from 5e-05 to 0.0005
- fast_in: bfloat16 [4, 640, 640], P('head'), may hold values from -0.25 to 0.25
- fast_gate: bfloat16 [4, 640, 640], P('head'), may hold values from -0.25 to 0.25
- fast_out: bfloat16 [4, 640, 640], P('head'), may hold values from -0.25 to 0.25
- head_gain: float32 [2560], P('head'), may hold values from 0.1 to 1.9
- out_proj: bfloat16 [2560, 2560], P('head', 'ctx'), may hold values from -0.15625 to 0.15625
Outputs:
- output: bfloat16 [16384, 2560], P('ctx', 'head')
- new_in: bfloat16 [4, 640, 640], P('head')
- new_gate: bfloat16 [4, 640, 640], P('head')
- new_out: bfloat16 [4, 640, 640], P('head')
The draws below stay inside these ranges and needn't reach their ends.
All inputs are finite; a program needn't handle non-finite values.
Results may differ from the reference program's by a relative error of at most 0.012.
Values may be sent and summed in bfloat16 or wider, within the bound.
No kernel may reach another device: no remote copies, remote signals or barrier semaphores. Data moves between devices by JAX's collectives and lax.ppermute only.
A program may use at most 128 MiB of HBM per device.

```python
import math
import jax
import jax.numpy as jnp
from jax import lax

D = 2560
HEADS = 4
DH = 640
DFF = 640
TOKENS = 16384


def raised(result, stream_key, source, target, shards_of, factor):
    def block_of(axis_at):
        return (jnp.arange(result.shape[axis_at]) // (result.shape[axis_at] // shards_of)).reshape((-1,) + (1,) * (result.ndim - 1 - axis_at))

    first = jax.random.permutation(stream_key, shards_of)[block_of(target)]
    far = (block_of(target) + shards_of // 2) % shards_of
    return jnp.where((block_of(source) == first) | (block_of(source) == far), factor * result, result)


def block_scale(key, extent, split, low, top_value):
    def one(axis_at, blocks):
        heights = jax.random.uniform(jax.random.fold_in(jax.random.fold_in(key, 6), axis_at), (blocks,), jnp.float32, low / len(split), top_value / len(split))
        return jnp.repeat(jnp.exp(heights), extent[axis_at] // blocks).reshape((-1,) + (1,) * (len(extent) - axis_at - 1))

    loudness = one(*split[0])
    for cut in split[1:]:
        loudness = loudness * one(*cut)
    return loudness


def noise(rng, extent, deviation, limit, cuts=(), kind=jnp.bfloat16):
    drawn = deviation * jax.random.normal(rng, extent, jnp.float32)
    if cuts:
        drawn = drawn * block_scale(rng, extent, cuts, -0.22, 0.18)
    return jnp.clip(drawn, -limit, limit).astype(kind)


def heavy_noise(own_key, extent, spread, reach, pieces, heavy, dtype=jnp.bfloat16):
    result = spread * jax.random.normal(own_key, extent, jnp.float32)
    if pieces:
        result = result * block_scale(own_key, extent, pieces, -0.22, 0.18)
    return jnp.clip(raised(result, jax.random.fold_in(own_key, 3), *heavy), -reach, reach).astype(dtype)


def setup_inputs(seed: int = 0) -> dict:
    arg_keys = jax.random.split(jax.random.key(seed), 10)
    return {
        "key_rows": noise(arg_keys[0], (TOKENS, D), 1.0, 6.0, ((0, 16), (1, 2))),
        "value_rows": noise(arg_keys[1], (TOKENS, D), 1.0, 6.0, ((0, 16), (1, 2))),
        "query_rows": noise(arg_keys[2], (TOKENS, D), 1.0, 6.0, ((0, 16), (1, 2))),
        "learn_rates": jnp.clip(jnp.exp(math.log(0.0005) - 2.3025852 * jax.random.uniform(arg_keys[3], (HEADS, TOKENS), jnp.float32) ** block_scale(arg_keys[3], (HEADS, TOKENS), ((0, 2), (1, 16)), -0.2, 0.2)), 4.999999873689376e-05, 0.0005),
        "fast_in": noise(arg_keys[4], (HEADS, DH, DFF), DH ** -0.5, 0.25, ((0, 2),)),
        "fast_gate": noise(arg_keys[5], (HEADS, DH, DFF), DH ** -0.5, 0.25, ((0, 2),)),
        "fast_out": noise(arg_keys[6], (HEADS, DFF, DH), DFF ** -0.5, 0.25, ((0, 2),)),
        "head_gain": jnp.clip(1.0 + 0.18 * jax.random.normal(arg_keys[7], (D,), jnp.float32), 0.1, 1.9),
        "out_proj": heavy_noise(arg_keys[8], (D, D), D ** -0.5, 0.15625, ((0, 2), (1, 16)), (0, 1, 16, 2.0)),
    }


def renorm(weight, grad):
    wide = weight.astype(jnp.float32)
    moved = wide - grad
    scale = jnp.sqrt(lax.optimization_barrier(jnp.sum(wide * wide, axis=0, keepdims=True)) + 1e-06) / jnp.sqrt(lax.optimization_barrier(jnp.sum(moved * moved, axis=0, keepdims=True)) + 1e-06)
    return (moved * scale).astype(jnp.bfloat16)

def reference(key_rows, value_rows, query_rows, learn_rates, fast_in, fast_gate, fast_out, head_gain, out_proj):
    new_ins = []
    new_gates = []
    new_outs = []
    normed_list = []
    for head_num in range(HEADS):
        lower = head_num * DH
        keyed = key_rows[:, lower:lower + DH]
        valued = value_rows[:, lower:lower + DH]
        queried = query_rows[:, lower:lower + DH]
        rate_col = learn_rates[head_num][:, None]
        pre_in = jnp.dot(keyed, fast_in[head_num], preferred_element_type=jnp.float32)
        pre_gate = jnp.dot(keyed, fast_gate[head_num], preferred_element_type=jnp.float32)
        sig = jax.nn.sigmoid(pre_in)
        act = pre_in * sig
        hidden = (act * pre_gate).astype(jnp.bfloat16)
        err = (-rate_col * valued.astype(jnp.float32)).astype(jnp.bfloat16)
        grad_out = jnp.dot(hidden.T, err, preferred_element_type=jnp.float32)
        back = jnp.dot(err, fast_out[head_num].T, preferred_element_type=jnp.float32)
        back_in = (back * pre_gate * sig * (1.0 + pre_in * (1.0 - sig))).astype(jnp.bfloat16)
        back_gate = (back * act).astype(jnp.bfloat16)
        grad_in = jnp.dot(keyed.T, back_in, preferred_element_type=jnp.float32)
        grad_gate = jnp.dot(keyed.T, back_gate, preferred_element_type=jnp.float32)
        upd_in = renorm(fast_in[head_num], grad_in)
        upd_gate = renorm(fast_gate[head_num], grad_gate)
        upd_out = renorm(fast_out[head_num], grad_out)
        q_in = jnp.dot(queried, upd_in, preferred_element_type=jnp.float32)
        q_gate = jnp.dot(queried, upd_gate, preferred_element_type=jnp.float32)
        q_hidden = (jax.nn.silu(q_in) * q_gate).astype(jnp.bfloat16)
        head_out = jnp.dot(q_hidden, upd_out, preferred_element_type=jnp.float32)
        inverse = jax.lax.rsqrt(lax.optimization_barrier(jnp.mean(head_out * head_out, axis=-1, keepdims=True)) + 1e-06)
        normed_list.append((head_out * inverse * head_gain[lower:lower + DH]).astype(jnp.bfloat16))
        new_ins.append(upd_in)
        new_gates.append(upd_gate)
        new_outs.append(upd_out)
    normed = jnp.concatenate(normed_list, axis=1)
    output = jnp.dot(normed, out_proj, preferred_element_type=jnp.float32).astype(jnp.bfloat16)
    return (output, jnp.stack(new_ins), jnp.stack(new_gates), jnp.stack(new_outs))
```

```python
import functools

import jax
import jax.numpy as jnp
from jax import lax
from jax.experimental import pallas as pl
from jax.experimental.pallas import tpu as pltpu
from jax.sharding import PartitionSpec as P

F32 = jnp.float32
BF16 = jnp.bfloat16
NT = (((1,), (1,)), ((), ()))
EPS = 1e-06
VMEM_BYTES = 56 * 1024 * 1024
PARAMS = pltpu.CompilerParams(vmem_limit_bytes=VMEM_BYTES, dimension_semantics=("arbitrary",))


def dot(a, b):
    return jnp.dot(a, b, preferred_element_type=F32)


def dot_nt(a, b):
    return lax.dot_general(a, b, NT, preferred_element_type=F32)


def sigmoid(x):
    return 0.5 * jnp.tanh(0.5 * x) + 0.5


def grad_kernel(head_ref, k_ref, v_ref, lr_ref, win_ref, wgate_ref, wout_ref, pair_ref, out_ref, *refs):
    w_t, backs = refs[-2:]
    units = wout_ref.shape[1]
    w_t[0:units] = win_ref[0].T
    w_t[units:] = wgate_ref[0].T
    if len(refs) > 2:
        refs[0][...] = w_t[...].reshape(refs[0].shape)
        refs[1][...] = wout_ref[0].T
    k = k_ref[...]
    v = v_ref[...]
    rate = -lr_ref[pl.ds(head_ref[0], 1), :]
    count = units // 2
    for lo in range(0, units, count):
        pre_in = dot_nt(w_t[lo : lo + count], k)
        pre_gate = dot_nt(w_t[units + lo : units + lo + count], k)
        back = dot_nt(wout_ref[0, lo : lo + count], v) * rate
        sig = sigmoid(pre_in)
        act = pre_in * sig
        backs[lo : lo + count] = (back * pre_gate * (sig + act * (1.0 - sig))).astype(BF16)
        backs[units + lo : units + lo + count] = (back * act).astype(BF16)
        backs[2 * units + lo : 2 * units + lo + count] = (act * pre_gate * rate).astype(BF16)
    pair_ref[...] = dot(backs[0 : 2 * units], k).astype(BF16).reshape(pair_ref.shape)
    out_ref[...] = dot(backs[2 * units :], v).T.astype(BF16)


def grads_of(head, with_weights, key_rows, value_rows, learn_rates, fast_in, fast_gate, fast_out):
    tokens = key_rows.shape[0]
    heads, width, units = fast_in.shape
    weight = pl.BlockSpec((1, width, units), lambda t, h: (h[0], 0, 0))
    rows = pl.BlockSpec((tokens, width), lambda t, h: (0, h[0]))
    copies = 1 + with_weights
    return pl.pallas_call(
        grad_kernel,
        out_shape=[jax.ShapeDtypeStruct((2, units, width), BF16), jax.ShapeDtypeStruct((width, units), BF16)] * copies,
        grid_spec=pltpu.PrefetchScalarGridSpec(
            num_scalar_prefetch=1,
            grid=(1,),
            in_specs=[rows, rows, pl.BlockSpec((heads, tokens), lambda t, h: (0, 0)), weight, weight, weight],
            out_specs=[
                pl.BlockSpec((2, units, width), lambda t, h: (0, 0, 0)),
                pl.BlockSpec((width, units), lambda t, h: (0, 0)),
            ]
            * copies,
            scratch_shapes=[pltpu.VMEM((2 * units, width), BF16), pltpu.VMEM((3 * units, tokens), BF16)],
        ),
        compiler_params=PARAMS,
        cost_estimate=pl.CostEstimate(
            flops=tokens * width * units, bytes_accessed=4 * tokens * width, transcendentals=0
        ),
        name="grads",
    )(head, key_rows, value_rows, learn_rates, fast_in, fast_gate, fast_out)


def settle(spot_ref, pairs, outs, pair_scratch, out_scratch):
    sides, ranks, two, piece, _ = pairs.shape
    upper, rank = spot_ref[1], spot_ref[2]
    half = ranks * piece
    units = sides * half
    for s in range(sides):
        for r in range(ranks):
            start = (upper ^ s) * half + (rank ^ r) * piece
            for m in range(two):
                pair_scratch[pl.ds(pl.multiple_of(m * units + start, piece), piece), :] = pairs[s, r, m]
            start = (rank ^ r) * (sides * piece) + (upper ^ s) * piece
            out_scratch[pl.ds(pl.multiple_of(start, piece), piece), :] = outs[r, s]


def query_kernel(final, spot_ref, *refs):
    q_refs, gain_ref = refs[0:2], refs[2]
    earlier_ref = refs[7] if final else None
    proj_ref, out_ref, normed_ref, pair_scratch, out_scratch = refs[-5:]
    width = q_refs[0].shape[1]

    @pl.when(pl.program_id(0) == 0)
    def _():
        for j in range(2):
            settle(spot_ref, refs[3 + 2 * j], refs[4 + 2 * j], pair_scratch.at[j], out_scratch.at[j])

    for j in range(2):
        head = spot_ref[0] if j == 0 else 1 - spot_ref[0]
        both = dot_nt(q_refs[j][...], pair_scratch[j])
        units = both.shape[1] // 2
        q_in, q_gate = both[:, :units], both[:, units:]
        hidden = (q_in * sigmoid(q_in) * q_gate).astype(BF16)
        head_out = dot_nt(hidden, out_scratch[j])
        inverse = lax.rsqrt(jnp.mean(head_out * head_out, axis=-1, keepdims=True) + EPS)
        normed = (head_out * inverse * gain_ref[head]).astype(BF16)
        normed_ref[:, pl.ds(pl.multiple_of(head * width, 128), width)] = normed
    total = dot_nt(normed_ref[...], proj_ref[0])
    if final:
        total = total + earlier_ref[...]
    out_ref[...] = total.astype(out_ref.dtype)


def query_heads(spot, queries, gains, proj, mine, theirs, earlier):
    tokens = queries.shape[0]
    _, outs, lanes = proj.shape
    width = units = lanes // 2
    block = tokens // 2
    final = earlier is not None

    def whole(array):
        return pl.BlockSpec(array.shape, lambda t, s: (0,) * array.ndim)

    in_specs = [
        pl.BlockSpec((block, width), lambda t, s: (t, s[0])),
        pl.BlockSpec((block, width), lambda t, s: (t, 1 - s[0])),
        whole(gains),
    ] + [whole(a) for a in (*mine, *theirs)]
    operands = [queries, queries, gains, *mine, *theirs]
    if final:
        in_specs.append(pl.BlockSpec((block, outs), lambda t, s: (t, 0)))
        operands.append(earlier)
    in_specs.append(pl.BlockSpec((1, outs, lanes), lambda t, s: (s[3], 0, 0)))
    operands.append(proj)
    return pl.pallas_call(
        functools.partial(query_kernel, final),
        out_shape=jax.ShapeDtypeStruct((tokens, outs), BF16 if final else F32),
        grid_spec=pltpu.PrefetchScalarGridSpec(
            num_scalar_prefetch=1,
            grid=(tokens // block,),
            in_specs=in_specs,
            out_specs=pl.BlockSpec((block, outs), lambda t, s: (t, 0)),
            scratch_shapes=[
                pltpu.VMEM((block, lanes), BF16),
                pltpu.VMEM((2, 2 * units, width), BF16),
                pltpu.VMEM((2, width, units), BF16),
            ],
        ),
        compiler_params=PARAMS,
        cost_estimate=pl.CostEstimate(
            flops=12 * tokens * width * width + 4 * tokens * width * outs,
            bytes_accessed=4 * tokens * width + 12 * width * width + 4 * tokens * outs,
            transcendentals=0,
        ),
        name="queries",
    )(spot, *operands)


def untranspose_kernel(spot_ref, *refs):
    outs, pair_scratch, out_scratch = refs[4:7], refs[7], refs[8]
    units = out_scratch.shape[1]
    for j in range(2):

        @pl.when(pl.program_id(0) == j)
        def _():
            settle(spot_ref, refs[2 * j], refs[2 * j + 1], pair_scratch, out_scratch)

    outs[0][0] = pair_scratch[0:units].T
    outs[1][0] = pair_scratch[units:].T
    outs[2][0] = out_scratch[...].T


def untransposed(spot, mine, theirs):
    width = mine[0].shape[-1]
    units = width

    def whole(array):
        return pl.BlockSpec(array.shape, lambda j, s: (0,) * array.ndim)

    return pl.pallas_call(
        untranspose_kernel,
        out_shape=[jax.ShapeDtypeStruct((2, width, units), BF16)] * 3,
        grid_spec=pltpu.PrefetchScalarGridSpec(
            num_scalar_prefetch=1,
            grid=(2,),
            in_specs=[whole(a) for a in (*mine, *theirs)],
            out_specs=[pl.BlockSpec((1, width, units), lambda j, s: (j + s[0] - 2 * j * s[0], 0, 0))] * 3,
            scratch_shapes=[pltpu.VMEM((2 * units, width), BF16), pltpu.VMEM((width, units), BF16)],
        ),
        compiler_params=PARAMS,
        cost_estimate=pl.CostEstimate(flops=0, bytes_accessed=24 * units * width, transcendentals=0),
        name="untranspose",
    )(spot, *mine, *theirs)


def renorm(wide, grad):
    moved = wide - grad
    scale = jnp.sqrt(jnp.sum(wide * wide, axis=-1, keepdims=True) + EPS) / jnp.sqrt(
        jnp.sum(moved * moved, axis=-1, keepdims=True) + EPS
    )
    return (moved * scale).astype(BF16)


def on_device(n_ctx, n_head, key_rows, value_rows, query_rows, learn_rates, fast_in, fast_gate, fast_out, head_gain, out_proj):
    heads, width, units = fast_in.shape
    place = lax.axis_index("ctx")
    group = lax.axis_index("head")
    core, upper, rank = place % 2, (place // 2) % 2, place // 4
    ranks = n_ctx // 4
    half = units // 2
    piece = half // ranks

    def across(array, mask):
        return lax.ppermute(array, "ctx", [(j, j ^ mask) for j in range(n_ctx)])

    def over(array):
        return lax.ppermute(array, "head", [(j, j ^ 1) for j in range(n_head)])

    def part(array, start, count, axis=0):
        return lax.dynamic_slice_in_dim(array, start, count, axis)

    def to_upper(array_for):
        return across(array_for(1 - upper), 2)

    def to_ranks(array_for):
        return [across(array_for(rank ^ d), 4 * d) for d in range(1, ranks)]

    tie = lax.optimization_barrier

    core_arg = core.astype(jnp.int32).reshape(1)
    inputs = (key_rows, value_rows, learn_rates, fast_in, fast_gate, fast_out)

    tokens = query_rows.shape[0]
    third = tokens // 3 // 16 * 16
    cuts = (0, tokens - 2 * third, tokens - third, tokens)
    query_parts = [query_rows[a:b] for a, b in zip(cuts, cuts[1:])]
    far_parts = [over(query_parts[0])]
    far_gain = over(head_gain)

    half_ctx = n_ctx // 2
    here = (place // half_ctx) == group
    block = out_proj.T
    pairs = []
    for j in range(half_ctx):
        low, high = (j * n_head) + 1, (j + half_ctx) * n_head
        pairs += [(low, high), (high, low)]
    swapped = lax.ppermute(block, ("ctx", "head"), pairs)

    other = grads_of(1 - core_arg, 0, *inputs)
    other, inputs, far_gain = tie((other, inputs, far_gain))
    got_pair, got_out = (across(a, 1) for a in other)
    own_pair, own_out, pair_old, out_old = grads_of(core_arg, 1, *inputs)
    own_pair, own_out, swapped = tie((own_pair, own_out, swapped))
    proj = lax.all_gather(jnp.where(here, block, swapped), "ctx", axis=0, tiled=True)
    proj = proj.reshape(2, -1, proj.shape[1])

    def pair_sum(start, count):
        return part(own_pair, start, count, 1).astype(F32) + part(got_pair, start, count, 1).astype(F32)

    def out_sum(start, count):
        return part(own_out, start, count).astype(F32) + part(got_out, start, count).astype(F32)

    pair_got = to_upper(lambda u: pair_sum(u * half, half).astype(BF16))
    out_got = to_ranks(lambda r: out_sum(r * 2 * piece, 2 * piece).astype(BF16))
    pair_total = pair_sum(upper * half, half) + pair_got.astype(F32)
    out_total = out_sum(rank * 2 * piece, 2 * piece)
    for a in out_got:
        out_total = out_total + a.astype(F32)
    pair_sent, out_sent = pair_total.astype(BF16), out_total.astype(BF16)
    pair_sent, out_sent, far_parts[0], query_parts = tie((pair_sent, out_sent, far_parts[0], query_parts))
    pair_got = to_ranks(lambda r: part(pair_sent, r * piece, piece, 1))
    out_got = to_upper(lambda u: part(out_sent, u * piece, piece))
    far_parts.append(over(query_parts[1]))
    pair_grad = part(pair_total, rank * piece, piece, 1)
    for a in pair_got:
        pair_grad = pair_grad + a.astype(F32)
    out_grad = part(out_total, upper * piece, piece) + out_got.astype(F32)

    pair_wide = part(pair_old, upper * half + rank * piece, piece, 1).astype(F32)
    out_wide = part(out_old, rank * 2 * piece + upper * piece, piece).astype(F32)
    pair_new, out_new = renorm(pair_wide, pair_grad), renorm(out_wide, out_grad)
    pair_new, out_new, far_parts[1], query_parts = tie((pair_new, out_new, far_parts[1], query_parts))

    pair_held = jnp.stack([pair_new] + to_ranks(lambda r: pair_new))
    out_held = jnp.stack([out_new, to_upper(lambda u: out_new)])
    far_parts.append(over(query_parts[2]))
    pair_held, out_held, far_parts = tie((pair_held, out_held, far_parts))

    def finish(pair, out, beside):
        pair_got, out_got = across(pair, 2), to_ranks(lambda r: out)
        pair_got, out_got, done = tie((pair_got, out_got, beside()))
        return (jnp.stack([pair, pair_got]), jnp.stack([out] + out_got)), done

    if piece % 16:
        spot = jnp.stack([core, 0, 0, 0]).astype(jnp.int32)
    else:
        spot = jnp.stack([core, upper, rank, 0]).astype(jnp.int32)
    spot, far_spot = spot.at[3].set(group), spot.at[3].set(1 - group)

    def settled(pair, out):
        if piece % 16:
            side, order = jnp.arange(2) ^ upper, jnp.arange(ranks) ^ rank
            pair = jnp.take(jnp.take(pair, side, 0), order, 1).transpose(2, 0, 1, 3, 4).reshape(1, 1, 2, units, width)
            out = jnp.take(jnp.take(out, order, 0), side, 1).reshape(1, 1, units, width)
        return pair, out

    shards = pair_held.size // pair_new[0].size
    both = jnp.concatenate([pair_held.reshape(shards, piece, width), out_held])
    mine, both = finish(pair_held, out_held, lambda: over(both))
    far_pair, far_out = both[:shards].reshape(pair_held.shape), both[shards:]
    theirs = tuple(across(a, 1) for a in mine)
    mine, theirs, far_pair, far_out = tie((mine, theirs, far_pair, far_out))

    gains = head_gain.reshape(heads, 1, width)
    far_gains = far_gain.reshape(heads, 1, width)
    far_mine, partial = finish(
        far_pair,
        far_out,
        lambda: query_heads(spot, query_rows, gains, proj, settled(*mine), settled(*theirs), None),
    )
    mine, theirs, far_mine = tie((mine, theirs, far_mine))
    far_theirs = tuple(across(a, 1) for a in far_mine)
    news = untransposed(spot, settled(*mine), settled(*theirs))
    far_rows = jnp.concatenate(far_parts)
    output = query_heads(far_spot, far_rows, far_gains, proj, settled(*far_mine), settled(*far_theirs), partial)
    return (output, *news)


def solution(mesh):
    return jax.shard_map(
        functools.partial(on_device, mesh.shape["ctx"], mesh.shape["head"]),
        mesh=mesh,
        in_specs=(
            P("ctx", "head"),
            P("ctx", "head"),
            P("ctx", "head"),
            P("head", "ctx"),
            P("head", None, None),
            P("head", None, None),
            P("head", None, None),
            P("head"),
            P("head", "ctx"),
        ),
        out_specs=(
            P("ctx", "head"),
            P("head", None, None),
            P("head", None, None),
            P("head", None, None),
        ),
        check_vma=False,
    )
```

```python
import functools

import jax
import jax.numpy as jnp
from jax import lax
from jax.experimental import pallas as pl
from jax.experimental.pallas import tpu as pltpu
from jax.sharding import PartitionSpec as P

F32 = jnp.float32
BF16 = jnp.bfloat16
NT = (((1,), (1,)), ((), ()))
EPS = 1e-06
VMEM_BYTES = 56 * 1024 * 1024
PARAMS = pltpu.CompilerParams(vmem_limit_bytes=VMEM_BYTES, dimension_semantics=("arbitrary",))


def dot(a, b):
    return jnp.dot(a, b, preferred_element_type=F32)


def dot_nt(a, b):
    return lax.dot_general(a, b, NT, preferred_element_type=F32)


def sigmoid(x):
    return 0.5 * jnp.tanh(0.5 * x) + 0.5


def grad_kernel(head_ref, k_ref, v_ref, lr_ref, win_ref, wgate_ref, wout_ref, pair_ref, out_ref, *refs):
    w_t, backs = refs[-2:]
    units = wout_ref.shape[1]
    w_t[0:units] = win_ref[0].T
    w_t[units:] = wgate_ref[0].T
    if len(refs) > 2:
        refs[0][...] = w_t[...].reshape(refs[0].shape)
        refs[1][...] = wout_ref[0].T
    k = k_ref[...]
    v = v_ref[...]
    rate = -lr_ref[pl.ds(head_ref[0], 1), :]
    count = units // 2
    for lo in range(0, units, count):
        pre_in = dot_nt(w_t[lo : lo + count], k)
        pre_gate = dot_nt(w_t[units + lo : units + lo + count], k)
        back = dot_nt(wout_ref[0, lo : lo + count], v) * rate
        sig = sigmoid(pre_in)
        act = pre_in * sig
        backs[lo : lo + count] = (back * pre_gate * (sig + act * (1.0 - sig))).astype(BF16)
        backs[units + lo : units + lo + count] = (back * act).astype(BF16)
        backs[2 * units + lo : 2 * units + lo + count] = (act * pre_gate * rate).astype(BF16)
    pair_ref[...] = dot(backs[0 : 2 * units], k).astype(BF16).reshape(pair_ref.shape)
    out_ref[...] = dot(backs[2 * units :], v).T.astype(BF16)


def grads_of(head, with_weights, key_rows, value_rows, learn_rates, fast_in, fast_gate, fast_out):
    tokens = key_rows.shape[0]
    heads, width, units = fast_in.shape
    weight = pl.BlockSpec((1, width, units), lambda t, h: (h[0], 0, 0))
    rows = pl.BlockSpec((tokens, width), lambda t, h: (0, h[0]))
    copies = 1 + with_weights
    return pl.pallas_call(
        grad_kernel,
        out_shape=[jax.ShapeDtypeStruct((2, units, width), BF16), jax.ShapeDtypeStruct((width, units), BF16)] * copies,
        grid_spec=pltpu.PrefetchScalarGridSpec(
            num_scalar_prefetch=1,
            grid=(1,),
            in_specs=[rows, rows, pl.BlockSpec((heads, tokens), lambda t, h: (0, 0)), weight, weight, weight],
            out_specs=[
                pl.BlockSpec((2, units, width), lambda t, h: (0, 0, 0)),
                pl.BlockSpec((width, units), lambda t, h: (0, 0)),
            ]
            * copies,
            scratch_shapes=[pltpu.VMEM((2 * units, width), BF16), pltpu.VMEM((3 * units, tokens), BF16)],
        ),
        compiler_params=PARAMS,
        cost_estimate=pl.CostEstimate(
            flops=tokens * width * units, bytes_accessed=4 * tokens * width, transcendentals=0
        ),
        name="grads",
    )(head, key_rows, value_rows, learn_rates, fast_in, fast_gate, fast_out)


def settle(spot_ref, pair_refs, out_refs, pair_scratch, out_scratch):
    upper, rank = spot_ref[1], spot_ref[2]
    pairs = [r.at[s] for r in pair_refs for s in range(r.shape[0])]
    outs = [r.at[s] for r in out_refs for s in range(r.shape[0])]
    sides, (ranks, two, piece, _) = len(pairs), pairs[0].shape
    half = ranks * piece
    units = sides * half
    for s in range(sides):
        for r in range(ranks):
            start = (upper ^ s) * half + (rank ^ r) * piece
            for m in range(two):
                pair_scratch[pl.ds(pl.multiple_of(m * units + start, piece), piece), :] = pairs[s][r, m]
            start = (rank ^ r) * (sides * piece) + (upper ^ s) * piece
            out_scratch[pl.ds(pl.multiple_of(start, piece), piece), :] = outs[r][s]


def taken(refs, counts):
    groups, at = [], 0
    for c in counts:
        groups.append(refs[at : at + c])
        at += c
    return groups


def query_kernel(counts, masks, final, spot_ref, *refs):
    *groups, rest = taken(refs, (*counts, len(refs) - sum(counts)))
    q_refs, proj_refs, weight_refs = groups[0], groups[1], groups[2:6]
    gain_ref = rest[0]
    earlier_ref = rest[1] if final else None
    out_ref, normed_ref, pair_scratch, out_scratch, proj_scratch, q_scratch = rest[-6:]
    block, lanes = normed_ref.shape
    width = lanes // 2

    @pl.when(pl.program_id(0) == 0)
    def _():
        for j in range(2):
            settle(spot_ref, weight_refs[2 * j], weight_refs[2 * j + 1], pair_scratch.at[j], out_scratch.at[j])
        rows = proj_refs[0].shape[2]
        for ref, mask in zip(proj_refs, masks):
            for k, m in enumerate(mask):
                start = pl.multiple_of((spot_ref[3] ^ m) * rows, rows)
                for j in range(2):
                    proj_scratch[pl.ds(start, rows), j * width : (j + 1) * width] = ref[k, j]
        at = 0
        for ref in q_refs:
            q_scratch[at : at + ref.shape[0]] = ref[...]
            at += ref.shape[0]

    here = pl.ds(pl.multiple_of(pl.program_id(0) * block, block), block)
    for j in range(2):
        head = spot_ref[0] if j == 0 else 1 - spot_ref[0]
        columns = pl.ds(pl.multiple_of(head * width, 128), width)
        both = dot_nt(q_scratch[here, columns], pair_scratch[j])
        units = both.shape[1] // 2
        q_in, q_gate = both[:, :units], both[:, units:]
        hidden = (q_in * sigmoid(q_in) * q_gate).astype(BF16)
        head_out = dot_nt(hidden, out_scratch[j])
        inverse = lax.rsqrt(jnp.mean(head_out * head_out, axis=-1, keepdims=True) + EPS)
        normed_ref[:, columns] = (head_out * inverse * gain_ref[head]).astype(BF16)
    total = dot_nt(normed_ref[...], proj_scratch[...])
    if final:
        total = total + earlier_ref[...]
    out_ref[...] = total.astype(out_ref.dtype)


def whole(array):
    return pl.BlockSpec(array.shape, lambda t, s: (0,) * array.ndim, pipeline_mode=pl.Buffered(1))


def query_heads(spot, queries, gains, proj, masks, mine, theirs, earlier):
    tokens = sum(q.shape[0] for q in queries)
    lanes = queries[0].shape[1]
    width = units = lanes // 2
    outs = sum(len(m) for m in masks) * proj[0].shape[2]
    block = tokens // 2
    final = earlier is not None
    groups = (queries, proj, *mine, *theirs)
    counts = tuple(len(g) for g in groups)
    operands = [a for g in groups for a in g] + [gains]
    in_specs = [whole(a) for a in operands]
    if final:
        in_specs.append(pl.BlockSpec((block, outs), lambda t, s: (t, 0)))
        operands.append(earlier)
    return pl.pallas_call(
        functools.partial(query_kernel, counts, masks, final),
        out_shape=jax.ShapeDtypeStruct((tokens, outs), BF16 if final else F32),
        grid_spec=pltpu.PrefetchScalarGridSpec(
            num_scalar_prefetch=1,
            grid=(tokens // block,),
            in_specs=in_specs,
            out_specs=pl.BlockSpec((block, outs), lambda t, s: (t, 0)),
            scratch_shapes=[
                pltpu.VMEM((block, lanes), BF16),
                pltpu.VMEM((2, 2 * units, width), BF16),
                pltpu.VMEM((2, width, units), BF16),
                pltpu.VMEM((outs, lanes), BF16),
                pltpu.VMEM((tokens, lanes), BF16),
            ],
        ),
        compiler_params=PARAMS,
        cost_estimate=pl.CostEstimate(
            flops=12 * tokens * width * width + 4 * tokens * width * outs,
            bytes_accessed=4 * tokens * width + 12 * width * width + 4 * tokens * outs,
            transcendentals=0,
        ),
        name="queries",
    )(spot, *operands)


def untranspose_kernel(counts, spot_ref, *refs):
    *groups, rest = taken(refs, (*counts, len(refs) - sum(counts)))
    outs, pair_scratch, out_scratch = rest[0:3], rest[3], rest[4]
    units = out_scratch.shape[1]
    for j in range(2):

        @pl.when(pl.program_id(0) == j)
        def _():
            settle(spot_ref, groups[2 * j], groups[2 * j + 1], pair_scratch, out_scratch)

    outs[0][0] = pair_scratch[0:units].T
    outs[1][0] = pair_scratch[units:].T
    outs[2][0] = out_scratch[...].T


def untransposed(spot, mine, theirs):
    groups = (*mine, *theirs)
    operands = [a for g in groups for a in g]
    width = units = operands[0].shape[-1]
    return pl.pallas_call(
        functools.partial(untranspose_kernel, tuple(len(g) for g in groups)),
        out_shape=[jax.ShapeDtypeStruct((2, width, units), BF16)] * 3,
        grid_spec=pltpu.PrefetchScalarGridSpec(
            num_scalar_prefetch=1,
            grid=(2,),
            in_specs=[whole(a) for a in operands],
            out_specs=[pl.BlockSpec((1, width, units), lambda j, s: (j + s[0] - 2 * j * s[0], 0, 0))] * 3,
            scratch_shapes=[pltpu.VMEM((2 * units, width), BF16), pltpu.VMEM((width, units), BF16)],
        ),
        compiler_params=PARAMS,
        cost_estimate=pl.CostEstimate(flops=0, bytes_accessed=24 * units * width, transcendentals=0),
        name="untranspose",
    )(spot, *operands)


def renorm(wide, grad):
    moved = wide - grad
    scale = jnp.sqrt(jnp.sum(wide * wide, axis=-1, keepdims=True) + EPS) / jnp.sqrt(
        jnp.sum(moved * moved, axis=-1, keepdims=True) + EPS
    )
    return (moved * scale).astype(BF16)


def on_device(n_ctx, n_head, key_rows, value_rows, query_rows, learn_rates, fast_in, fast_gate, fast_out, head_gain, out_proj):
    heads, width, units = fast_in.shape
    place = lax.axis_index("ctx")
    group = lax.axis_index("head")
    core, upper, rank = place % 2, (place // 2) % 2, place // 4
    ranks = n_ctx // 4
    half = units // 2
    piece = half // ranks

    def across(array, mask):
        return lax.ppermute(array, "ctx", [(j, j ^ mask) for j in range(n_ctx)])

    def over(array):
        return lax.ppermute(array, "head", [(j, j ^ 1) for j in range(n_head)])

    def part(array, start, count, axis=0):
        return lax.dynamic_slice_in_dim(array, start, count, axis)

    def joined(array, rider):
        flat = array.reshape(-1, width)
        return flat if rider is None else jnp.concatenate([flat, rider])

    def parted(array, like, rider):
        count = like.size // width
        return array[:count].reshape(like.shape), None if rider is None else array[count:]

    def to_upper(array_for, rider=None):
        array = array_for(1 - upper)
        return parted(across(joined(array, rider), 2), array, rider)

    def to_ranks(array_for, rider=None):
        sent = [array_for(rank ^ d) for d in range(1, ranks)]
        first, rider = parted(across(joined(sent[0], rider), 4), sent[0], rider)
        return [first] + [across(a, 4 * d) for d, a in enumerate(sent[1:], 2)], rider

    tie = lax.optimization_barrier
    core_arg = core.astype(jnp.int32).reshape(1)
    inputs = (key_rows, value_rows, learn_rates, fast_in, fast_gate, fast_out)

    tokens = query_rows.shape[0]
    third = tokens // 3 // 16 * 16
    cuts = (0, tokens - 2 * third, tokens - third, tokens)
    query_parts = [query_rows[a:b] for a, b in zip(cuts, cuts[1:])]
    far_parts = [over(query_parts[0])]

    half_ctx = n_ctx // 2
    here = (place // half_ctx) == group
    rows = out_proj.shape[1]
    stepwise = ranks == 4 and rows % 16 == 0
    block = out_proj.T.reshape(rows, 2, width).transpose(1, 0, 2).reshape(2 * rows, width)
    if stepwise:
        blocks = [block, across(block, 4), across(block, 8)]
    else:
        pairs = []
        for j in range(half_ctx):
            low, high = (j * n_head) + 1, (j + half_ctx) * n_head
            pairs += [(low, high), (high, low)]
        swapped = lax.ppermute(out_proj.T, ("ctx", "head"), pairs)
        proj = lax.all_gather(jnp.where(here, out_proj.T, swapped), "ctx", axis=0, tiled=True)
        proj = proj.reshape(2, -1, 2, width).transpose(0, 2, 1, 3)
        blocks = []

    other = grads_of(1 - core_arg, 0, *inputs)
    other, inputs = tie((other, inputs))
    got_pair, got_out = (across(a, 1) for a in other)
    own_pair, own_out, pair_old, out_old = grads_of(core_arg, 1, *inputs)
    own_pair, own_out, blocks, far_parts, query_parts = tie((own_pair, own_out, blocks, far_parts, query_parts))
    far_parts.append(over(query_parts[1]))

    def pair_sum(start, count):
        return part(own_pair, start, count, 1).astype(F32) + part(got_pair, start, count, 1).astype(F32)

    def out_sum(start, count):
        return part(own_out, start, count).astype(F32) + part(got_out, start, count).astype(F32)

    pair_got, _ = to_upper(lambda u: pair_sum(u * half, half).astype(BF16))
    out_got, rider = to_ranks(
        lambda r: out_sum(r * 2 * piece, 2 * piece).astype(BF16), blocks[2] if stepwise else None
    )
    pair_total = pair_sum(upper * half, half) + pair_got.astype(F32)
    out_total = out_sum(rank * 2 * piece, 2 * piece)
    for a in out_got:
        out_total = out_total + a.astype(F32)
    pair_sent, out_sent = pair_total.astype(BF16), out_total.astype(BF16)
    kept = given = None
    if stepwise:
        near, away = jnp.concatenate(blocks[:2]), jnp.concatenate([blocks[2], rider])
        kept, given = jnp.where(here, near, away), jnp.where(here, away, near)
    pair_sent, out_sent, kept, given, far_parts = tie((pair_sent, out_sent, kept, given, far_parts))
    pair_got, _ = to_ranks(lambda r: part(pair_sent, r * piece, piece, 1))
    out_got, kept_upper = to_upper(lambda u: part(out_sent, u * piece, piece), kept)
    come = over(given) if stepwise else None
    pair_grad = part(pair_total, rank * piece, piece, 1)
    for a in pair_got:
        pair_grad = pair_grad + a.astype(F32)
    out_grad = part(out_total, upper * piece, piece) + out_got.astype(F32)
    pair_wide = part(pair_old, upper * half + rank * piece, piece, 1).astype(F32)
    out_wide = part(out_old, rank * 2 * piece + upper * piece, piece).astype(F32)
    pair_new, out_new = renorm(pair_wide, pair_grad), renorm(out_wide, out_grad)
    pair_new, out_new, come, query_parts = tie((pair_new, out_new, come, query_parts))

    pair_got, _ = to_ranks(lambda r: pair_new)
    out_got, come_upper = to_upper(lambda u: out_new, come)
    far_parts.append(over(query_parts[2]))
    pair_held, out_held = jnp.stack([pair_new] + pair_got), jnp.stack([out_new, out_got])
    if stepwise:
        masks = [[0, 4], [2, 6], [1, 5], [3, 7]]
        own_proj = [kept, kept_upper, across(kept, 1), across(kept_upper, 1)]
        come_core = across(come, 1)
    else:
        masks = [[0]]
        own_proj, far_proj = [part(proj, group, 1)], [part(proj, 1 - group, 1)]
        come_core = None
    pair_held, out_held, far_parts, own_proj, come_core = tie((pair_held, out_held, far_parts, own_proj, come_core))

    def finish(pair, out, beside):
        (pair_got, _), (out_got, _) = to_upper(lambda u: pair), to_ranks(lambda r: out)
        pair_got, out_got, done = tie((pair_got, out_got, beside()))
        return ([pair[None], pair_got[None]], [a[None] for a in (out, *out_got)]), done

    mine, far_pair = finish(pair_held, out_held, lambda: over(pair_held))
    mine = tuple([jnp.concatenate(g)] for g in mine)

    tiled = piece % 16 == 0
    spot = [core, upper, rank] if tiled else [core, 0, 0]
    spot = jnp.stack(spot + [place % half_ctx if stepwise else 0]).astype(jnp.int32)

    def settled(pair, out):
        if not tiled:
            side, order = jnp.arange(2) ^ upper, jnp.arange(ranks) ^ rank
            pair, out = jnp.concatenate(pair), jnp.concatenate(out)
            pair = jnp.take(jnp.take(pair, side, 0), order, 1).transpose(2, 0, 1, 3, 4).reshape(1, 1, 2, units, width)
            out = jnp.take(jnp.take(out, order, 0), side, 1).reshape(1, 1, units, width)
            pair, out = [pair], [out]
        return pair, out

    def swapped_cores(arrays):
        return [across(a, 1) for a in arrays]

    theirs = tuple(swapped_cores(g) for g in mine)
    if stepwise:
        far_proj = [come, come_upper, come_core, across(come_upper, 1)]
    mine, theirs, far_pair, far_out, far_proj = tie((mine, theirs, far_pair, over(out_held), far_proj))

    def blocks_of(arrays):
        return [a.reshape(-1, 2, rows, width) for a in arrays] if stepwise else arrays

    gains = head_gain.reshape(heads, 1, width)
    far_mine, (partial, far_gain, first_pair, first_out) = finish(
        far_pair,
        far_out,
        lambda: (
            query_heads(spot, [query_rows], gains, blocks_of(own_proj), masks, settled(*mine), settled(*theirs), None),
            over(head_gain),
            across(far_pair, 1),
            across(far_out, 1),
        ),
    )
    mine, theirs, far_mine = tie((mine, theirs, far_mine))
    far_theirs = [first_pair[None]] + swapped_cores(far_mine[0][1:]), [first_out[None]] + swapped_cores(far_mine[1][1:])
    far_gains = far_gain.reshape(heads, 1, width)
    news = untransposed(spot, settled(*mine), settled(*theirs))
    output = query_heads(
        spot, far_parts, far_gains, blocks_of(far_proj), masks, settled(*far_mine), settled(*far_theirs), partial
    )
    return (output, *news)


def solution(mesh):
    return jax.shard_map(
        functools.partial(on_device, mesh.shape["ctx"], mesh.shape["head"]),
        mesh=mesh,
        in_specs=(
            P("ctx", "head"),
            P("ctx", "head"),
            P("ctx", "head"),
            P("head", "ctx"),
            P("head", None, None),
            P("head", None, None),
            P("head", None, None),
            P("head"),
            P("head", "ctx"),
        ),
        out_specs=(
            P("ctx", "head"),
            P("head", None, None),
            P("head", None, None),
            P("head", None, None),
        ),
        check_vma=False,
    )
```

```python
import functools

import jax
import jax.numpy as jnp
from jax import lax
from jax.experimental import pallas as pl
from jax.experimental.pallas import tpu as pltpu
from jax.sharding import PartitionSpec as P

F32 = jnp.float32
BF16 = jnp.bfloat16
NT = (((1,), (1,)), ((), ()))
EPS = 1e-06
VMEM_BYTES = 56 * 1024 * 1024
PARAMS = pltpu.CompilerParams(vmem_limit_bytes=VMEM_BYTES, dimension_semantics=("arbitrary",))


def dot(a, b):
    return jnp.dot(a, b, preferred_element_type=F32)


def dot_nt(a, b):
    return lax.dot_general(a, b, NT, preferred_element_type=F32)


def sigmoid(x):
    return 0.5 * jnp.tanh(0.5 * x) + 0.5


def grad_kernel(far, spot_ref, k_ref, v_ref, lr_ref, win_ref, wgate_ref, wout_ref, pair_ref, out_ref, *refs):
    w_t, backs = refs[-2:]
    units = wout_ref.shape[1]
    w_t[0:units] = win_ref[0].T
    w_t[units:] = wgate_ref[0].T
    if len(refs) > 2:
        refs[0][...] = w_t[...].reshape(refs[0].shape)
        refs[1][...] = wout_ref[0].T
    k = k_ref[...]
    v = v_ref[...]
    rate = -lr_ref[pl.ds(1 - spot_ref[0] if far else spot_ref[0], 1), :]
    count = units // 2
    for lo in range(0, units, count):
        pre_in = dot_nt(w_t[lo : lo + count], k)
        pre_gate = dot_nt(w_t[units + lo : units + lo + count], k)
        back = dot_nt(wout_ref[0, lo : lo + count], v) * rate
        sig = sigmoid(pre_in)
        act = pre_in * sig
        backs[lo : lo + count] = (back * pre_gate * (sig + act * (1.0 - sig))).astype(BF16)
        backs[units + lo : units + lo + count] = (back * act).astype(BF16)
        backs[2 * units + lo : 2 * units + lo + count] = (act * pre_gate * rate).astype(BF16)
    pair_ref[...] = dot(backs[0 : 2 * units], k).astype(BF16).reshape(pair_ref.shape)
    out_ref[...] = dot(backs[2 * units :], v).T.astype(BF16)


def grads_of(spot, far, key_rows, value_rows, learn_rates, fast_in, fast_gate, fast_out):
    tokens = key_rows.shape[0]
    heads, width, units = fast_in.shape
    weight = pl.BlockSpec((1, width, units), lambda t, s: (1 - s[0] if far else s[0], 0, 0))
    rows = pl.BlockSpec((tokens, width), lambda t, s: (0, 1 - s[0] if far else s[0]))
    copies = 1 if far else 2
    return pl.pallas_call(
        functools.partial(grad_kernel, far),
        out_shape=[jax.ShapeDtypeStruct((2, units, width), BF16), jax.ShapeDtypeStruct((width, units), BF16)] * copies,
        grid_spec=pltpu.PrefetchScalarGridSpec(
            num_scalar_prefetch=1,
            grid=(1,),
            in_specs=[rows, rows, pl.BlockSpec((heads, tokens), lambda t, h: (0, 0)), weight, weight, weight],
            out_specs=[
                pl.BlockSpec((2, units, width), lambda t, h: (0, 0, 0)),
                pl.BlockSpec((width, units), lambda t, h: (0, 0)),
            ]
            * copies,
            scratch_shapes=[pltpu.VMEM((2 * units, width), BF16), pltpu.VMEM((3 * units, tokens), BF16)],
        ),
        compiler_params=PARAMS,
        cost_estimate=pl.CostEstimate(
            flops=tokens * width * units, bytes_accessed=4 * tokens * width, transcendentals=0
        ),
        name="grads",
    )(spot, key_rows, value_rows, learn_rates, fast_in, fast_gate, fast_out)


def taken(refs, counts):
    groups, at = [], 0
    for c in counts:
        groups.append(refs[at : at + c])
        at += c
    return groups


def query_kernel(counts, masks, final, spot_ref, *refs):
    *groups, rest = taken(refs, (*counts, len(refs) - sum(counts)))
    q_refs, proj_refs, weight_refs = groups[0], groups[1], groups[2:6]
    extra_ref, *outs, normed_ref, pair_scratch, out_scratch, proj_scratch, q_scratch, tail_scratch, sems = rest
    block, lanes = normed_ref.shape
    width = lanes // 2
    step = pl.program_id(0)
    upper, rank = spot_ref[1], spot_ref[2]

    def lined(start, count):
        return pl.ds(pl.multiple_of(start, count), count)

    copies = {}

    def plan(name, source, target):
        number = sum(len(c) for c in copies.values())
        copies.setdefault(name, []).append(pltpu.make_async_copy(source, target, sems.at[number]))

    at = 0
    for ref in q_refs:
        count = min(ref.shape[0], q_scratch.shape[0] - at)
        plan("q", ref.at[pl.ds(0, count)], q_scratch.at[pl.ds(at, count)])
        at += count
    if final:
        plan("q", q_refs[-1].at[pl.ds(q_refs[-1].shape[0] - 16, 16)], tail_scratch)
    for j in range(2):
        pairs = [r.at[s] for r in weight_refs[2 * j] for s in range(r.shape[0])]
        results = [r.at[s] for r in weight_refs[2 * j + 1] for s in range(r.shape[0])]
        sides, (ranks, _, piece, _) = len(pairs), pairs[0].shape
        for s in range(sides):
            for r in range(ranks):
                start = (upper ^ s) * (ranks * piece) + (rank ^ r) * piece
                plan(j, pairs[s].at[r], pair_scratch.at[j, :, lined(start, piece), :])
                start = (rank ^ r) * (sides * piece) + (upper ^ s) * piece
                plan(j, results[r].at[s], out_scratch.at[j, lined(start, piece), :])
    rows = proj_refs[0].shape[2]
    for ref, mask in zip(proj_refs, masks):
        for k, m in enumerate(mask):
            for j in range(2):
                target = proj_scratch.at[lined((spot_ref[3] ^ m) * rows, rows), pl.ds(j * width, width)]
                plan("proj", ref.at[k, j], target)

    @pl.when(step == 0)
    def _():
        for name in ("q", 0, 1, "proj"):
            for copy in copies[name]:
                copy.start()

    def arrived(*names):
        @pl.when(step == 0)
        def _():
            for name in names:
                for copy in copies[name]:
                    copy.wait()

    arrived("q", 0)
    if final:
        tail = tail_scratch[...].astype(F32)
        gains = tail[0:1] + tail[1:2] + tail[2:3]
    else:
        gains = extra_ref[...].reshape(1, lanes)
    for j in range(2):
        if j == 1:
            arrived(1)
        head = spot_ref[0] if j == 0 else 1 - spot_ref[0]
        columns = pl.ds(pl.multiple_of(head * width, 128), width)
        weights = pair_scratch[j]
        both = dot_nt(q_scratch[lined(step * block, block), columns], weights.reshape(-1, width))
        units = both.shape[1] // 2
        q_in, q_gate = both[:, :units], both[:, units:]
        hidden = (q_in * sigmoid(q_in) * q_gate).astype(BF16)
        head_out = dot_nt(hidden, out_scratch[j])
        inverse = lax.rsqrt(jnp.mean(head_out * head_out, axis=-1, keepdims=True) + EPS)
        gain = jnp.where(head == 0, gains[:, :width], gains[:, width:])
        normed_ref[:, columns] = (head_out * inverse * gain).astype(BF16)
    arrived("proj")
    total = dot_nt(normed_ref[...], proj_scratch[...])
    if final:
        total = total + extra_ref[...]
    else:
        outs[1][0] = pair_scratch[step, 0].T
        outs[2][0] = pair_scratch[step, 1].T
        outs[3][0] = out_scratch[step].T
    outs[0][...] = total.astype(outs[0].dtype)


def query_heads(spot, queries, gain, proj, masks, mine, theirs, earlier):
    final = earlier is not None
    tokens = sum(q.shape[0] for q in queries) - 16 * final
    lanes = queries[0].shape[1]
    width = units = lanes // 2
    outs = sum(len(m) for m in masks) * proj[0].shape[2]
    block = tokens // 2
    groups = (queries, proj, *mine, *theirs)
    counts = tuple(len(g) for g in groups)
    operands = [a for g in groups for a in g]
    in_specs = [pl.BlockSpec(memory_space=pl.ANY)] * len(operands)
    rows_spec = pl.BlockSpec((block, outs), lambda t, s: (t, 0))
    out_shape, out_specs = [jax.ShapeDtypeStruct((tokens, outs), BF16 if final else F32)], [rows_spec]
    if final:
        in_specs.append(rows_spec)
    else:
        in_specs.append(pl.BlockSpec(gain.shape, lambda t, s: (0,)))
        out_shape += [jax.ShapeDtypeStruct((2, width, units), BF16)] * 3
        out_specs += [pl.BlockSpec((1, width, units), lambda t, s: (t + s[0] - 2 * t * s[0], 0, 0))] * 3
    operands.append(earlier if final else gain)
    sides = sum(a.shape[0] for a in mine[0])
    ranks = sum(a.shape[0] for a in mine[1])
    copies = len(queries) + 1 + 4 * sides * ranks + 2 * sum(len(m) for m in masks)
    result = pl.pallas_call(
        functools.partial(query_kernel, counts, masks, final),
        out_shape=out_shape,
        grid_spec=pltpu.PrefetchScalarGridSpec(
            num_scalar_prefetch=1,
            grid=(tokens // block,),
            in_specs=in_specs,
            out_specs=out_specs,
            scratch_shapes=[
                pltpu.VMEM((block, lanes), BF16),
                pltpu.VMEM((2, 2, units, width), BF16),
                pltpu.VMEM((2, width, units), BF16),
                pltpu.VMEM((outs, lanes), BF16),
                pltpu.VMEM((tokens, lanes), BF16),
                pltpu.VMEM((16, lanes), BF16),
                pltpu.SemaphoreType.DMA((copies,)),
            ],
        ),
        compiler_params=PARAMS,
        cost_estimate=pl.CostEstimate(
            flops=12 * tokens * width * width + 4 * tokens * width * outs,
            bytes_accessed=4 * tokens * width + 12 * width * width + 4 * tokens * outs,
            transcendentals=0,
        ),
        name="queries",
    )(spot, *operands)
    return result[0] if final else result


def renorm(wide, grad):
    moved = wide - grad
    scale = jnp.sqrt(jnp.sum(wide * wide, axis=-1, keepdims=True) + EPS) / jnp.sqrt(
        jnp.sum(moved * moved, axis=-1, keepdims=True) + EPS
    )
    return (moved * scale).astype(BF16)


def on_device(n_ctx, n_head, key_rows, value_rows, query_rows, learn_rates, fast_in, fast_gate, fast_out, head_gain, out_proj):
    heads, width, units = fast_in.shape
    place = lax.axis_index("ctx")
    group = lax.axis_index("head")
    core, upper, rank = place % 2, (place // 2) % 2, place // 4
    ranks = n_ctx // 4
    half = units // 2
    piece = half // ranks

    def across(array, mask):
        return lax.ppermute(array, "ctx", [(j, j ^ mask) for j in range(n_ctx)])

    def over(array):
        return lax.ppermute(array, "head", [(j, j ^ 1) for j in range(n_head)])

    def part(array, start, count, axis=0):
        return lax.dynamic_slice_in_dim(array, start, count, axis)

    def joined(array, rider):
        flat = array.reshape(-1, width)
        return flat if rider is None else jnp.concatenate([flat, rider])

    def parted(array, like, rider):
        count = like.size // width
        return array[:count].reshape(like.shape), None if rider is None else array[count:]

    def to_upper(array_for, rider=None):
        array = array_for(1 - upper)
        return parted(across(joined(array, rider), 2), array, rider)

    def to_ranks(array_for, rider=None):
        sent = [array_for(rank ^ d) for d in range(1, ranks)]
        first, rider = parted(across(joined(sent[0], rider), 4), sent[0], rider)
        return [first] + [across(a, 4 * d) for d, a in enumerate(sent[1:], 2)], rider

    tie = lax.optimization_barrier
    inputs = (key_rows, value_rows, learn_rates, fast_in, fast_gate, fast_out)

    half_ctx = n_ctx // 2
    rows = out_proj.shape[1]
    stepwise = ranks == 4 and rows % 16 == 0
    tiled = piece % 16 == 0
    spot = [core, upper, rank] if tiled else [core, 0, 0]
    spot = jnp.stack(spot + [place % half_ctx if stepwise else 0]).astype(jnp.int32)

    tokens = query_rows.shape[0]
    third = tokens // 3 // 16 * 16
    cuts = (0, tokens - 2 * third, tokens - third, tokens)
    query_parts = [query_rows[a:b] for a, b in zip(cuts, cuts[1:])]
    far_parts = [over(query_parts[0])]
    high = lax.reduce_precision(head_gain, 8, 7)
    middle = lax.reduce_precision(head_gain - high, 8, 7)
    gain_rows = jnp.stack([high, middle, head_gain - high - middle]).astype(BF16)
    gain_rows = jnp.pad(gain_rows, ((0, 13), (0, 0)))

    here = (place // half_ctx) == group
    block = out_proj.T.reshape(rows, 2, width).transpose(1, 0, 2).reshape(2 * rows, width)
    if stepwise:
        blocks = [block, across(block, 4), across(block, 8)]
    else:
        pairs = []
        for j in range(half_ctx):
            low, high = (j * n_head) + 1, (j + half_ctx) * n_head
            pairs += [(low, high), (high, low)]
        swapped = lax.ppermute(out_proj.T, ("ctx", "head"), pairs)
        proj = lax.all_gather(jnp.where(here, out_proj.T, swapped), "ctx", axis=0, tiled=True)
        proj = proj.reshape(2, -1, 2, width).transpose(0, 2, 1, 3)
        blocks = []

    other = grads_of(spot, 1, *inputs)
    other, inputs, spot = tie((other, inputs, spot))
    got_pair, got_out = (across(a, 1) for a in other)
    own_pair, own_out, pair_old, out_old = grads_of(spot, 0, *inputs)
    own_pair, own_out, blocks, far_parts, query_parts = tie((own_pair, own_out, blocks, far_parts, query_parts))
    far_parts.append(over(query_parts[1]))

    def pair_sum(start, count):
        return part(own_pair, start, count, 1).astype(F32) + part(got_pair, start, count, 1).astype(F32)

    def out_sum(start, count):
        return part(own_out, start, count).astype(F32) + part(got_out, start, count).astype(F32)

    pair_got, _ = to_upper(lambda u: pair_sum(u * half, half).astype(BF16))
    out_got, rider = to_ranks(
        lambda r: out_sum(r * 2 * piece, 2 * piece).astype(BF16), blocks[2] if stepwise else None
    )
    pair_total = pair_sum(upper * half, half) + pair_got.astype(F32)
    out_total = out_sum(rank * 2 * piece, 2 * piece)
    for a in out_got:
        out_total = out_total + a.astype(F32)
    pair_sent, out_sent = pair_total.astype(BF16), out_total.astype(BF16)
    kept = given = None
    if stepwise:
        near, away = jnp.concatenate(blocks[:2]), jnp.concatenate([blocks[2], rider])
        kept, given = jnp.where(here, near, away), jnp.where(here, away, near)
    pair_sent, out_sent, kept, given, far_parts = tie((pair_sent, out_sent, kept, given, far_parts))
    pair_got, _ = to_ranks(lambda r: part(pair_sent, r * piece, piece, 1))
    out_got, kept_upper = to_upper(lambda u: part(out_sent, u * piece, piece), kept)
    come = over(given) if stepwise else None
    pair_grad = part(pair_total, rank * piece, piece, 1)
    for a in pair_got:
        pair_grad = pair_grad + a.astype(F32)
    out_grad = part(out_total, upper * piece, piece) + out_got.astype(F32)
    pair_wide = part(pair_old, upper * half + rank * piece, piece, 1).astype(F32)
    out_wide = part(out_old, rank * 2 * piece + upper * piece, piece).astype(F32)
    pair_new, out_new = renorm(pair_wide, pair_grad), renorm(out_wide, out_grad)
    pair_new, out_new, come, query_parts, kept, kept_upper = tie((pair_new, out_new, come, query_parts, kept, kept_upper))

    pair_got, _ = to_ranks(lambda r: pair_new)
    out_got, come_upper = to_upper(lambda u: out_new, come)
    far_parts.append(over(jnp.concatenate([query_parts[2], gain_rows])))
    far_new = over(out_new)
    pair_held, out_held = jnp.stack([pair_new] + pair_got), jnp.stack([out_new, out_got])
    pair_held, out_held, far_parts, far_new = tie((pair_held, out_held, far_parts, far_new))

    def finish(pair, out, beside, rider=None):
        (pair_got, rider), (out_got, _) = to_upper(lambda u: pair, rider), to_ranks(lambda r: out)
        pair_got, out_got, rider, done = tie((pair_got, out_got, rider, beside()))
        return ([pair[None], pair_got[None]], [a[None] for a in (out, *out_got)]), rider, done

    if stepwise:
        masks = [[0, 4, 2, 6], [1, 5, 3, 7]]
        own_proj = [jnp.concatenate([kept, kept_upper])]
        own_proj.append(across(own_proj[0], 1))
    else:
        masks = [[0]]
        own_proj, far_proj = [part(proj, group, 1)], [part(proj, 1 - group, 1)]
    mine, rider, far_pair = finish(pair_held, out_held, lambda: over(pair_held), far_new)
    far_out = jnp.stack([far_new, rider])
    mine = tuple([jnp.concatenate(g)] for g in mine)

    def settled(pair, out):
        if not tiled:
            side, order = jnp.arange(2) ^ upper, jnp.arange(ranks) ^ rank
            pair, out = jnp.concatenate(pair), jnp.concatenate(out)
            pair = jnp.take(jnp.take(pair, side, 0), order, 1).transpose(2, 0, 1, 3, 4).reshape(1, 1, 2, units, width)
            out = jnp.take(jnp.take(out, order, 0), side, 1).reshape(1, 1, units, width)
            pair, out = [pair], [out]
        return pair, out

    def swapped_cores(arrays):
        return [across(a, 1) for a in arrays]

    theirs = tuple(swapped_cores(g) for g in mine)
    if stepwise:
        far_proj = [jnp.concatenate([come, come_upper])]
        far_proj.append(across(far_proj[0], 1))
    mine, theirs = tie((mine, theirs))

    def blocks_of(arrays):
        return [a.reshape(-1, 2, rows, width) for a in arrays] if stepwise else arrays

    far_mine, _, ((partial, *news), far_proj) = finish(
        far_pair,
        far_out,
        lambda: (
            query_heads(
                spot, [query_rows], head_gain, blocks_of(own_proj), masks, settled(*mine), settled(*theirs), None
            ),
            far_proj,
        ),
    )
    far_theirs = tuple(swapped_cores(g) for g in far_mine)
    output = query_heads(
        spot, far_parts, None, blocks_of(far_proj), masks, settled(*far_mine), settled(*far_theirs), partial
    )
    return (output, *news)


def solution(mesh):
    return jax.shard_map(
        functools.partial(on_device, mesh.shape["ctx"], mesh.shape["head"]),
        mesh=mesh,
        in_specs=(
            P("ctx", "head"),
            P("ctx", "head"),
            P("ctx", "head"),
            P("head", "ctx"),
            P("head", None, None),
            P("head", None, None),
            P("head", None, None),
            P("head"),
            P("head", "ctx"),
        ),
        out_specs=(
            P("ctx", "head"),
            P("head", None, None),
            P("head", None, None),
            P("head", None, None),
        ),
        check_vma=False,
    )
```

```python
import functools

import jax
import jax.numpy as jnp
from jax import lax
from jax.experimental import pallas as pl
from jax.experimental.pallas import tpu as pltpu
from jax.sharding import PartitionSpec as P

F32 = jnp.float32
BF16 = jnp.bfloat16
NT = (((1,), (1,)), ((), ()))
EPS = 1e-06
VMEM_BYTES = 56 * 1024 * 1024
PARAMS = pltpu.CompilerParams(vmem_limit_bytes=VMEM_BYTES, dimension_semantics=("arbitrary",))


def dot(a, b):
    return jnp.dot(a, b, preferred_element_type=F32)


def dot_nt(a, b):
    return lax.dot_general(a, b, NT, preferred_element_type=F32)


def sigmoid(x):
    return 0.5 * jnp.tanh(0.5 * x) + 0.5


def grad_kernel(far, spot_ref, k_ref, v_ref, lr_ref, win_ref, wgate_ref, wout_ref, pair_ref, out_ref, *refs):
    w_t, backs = refs[-2:]
    units = wout_ref.shape[1]
    w_t[0:units] = win_ref[0].T
    w_t[units:] = wgate_ref[0].T
    if len(refs) > 2:
        refs[0][...] = w_t[...].reshape(refs[0].shape)
        refs[1][...] = wout_ref[0].T
    k = k_ref[...]
    v = v_ref[...]
    rate = -lr_ref[pl.ds(1 - spot_ref[0] if far else spot_ref[0], 1), :]
    count = units // 2
    for lo in range(0, units, count):
        pre_in = dot_nt(w_t[lo : lo + count], k)
        pre_gate = dot_nt(w_t[units + lo : units + lo + count], k)
        back = dot_nt(wout_ref[0, lo : lo + count], v) * rate
        sig = sigmoid(pre_in)
        act = pre_in * sig
        backs[lo : lo + count] = (back * pre_gate * (sig + act * (1.0 - sig))).astype(BF16)
        backs[units + lo : units + lo + count] = (back * act).astype(BF16)
        backs[2 * units + lo : 2 * units + lo + count] = (act * pre_gate * rate).astype(BF16)
    pair_ref[...] = dot(backs[0 : 2 * units], k).astype(BF16).reshape(pair_ref.shape)
    out_ref[...] = dot(backs[2 * units :], v).T.astype(BF16)


def grads_of(spot, far, key_rows, value_rows, learn_rates, fast_in, fast_gate, fast_out):
    tokens = key_rows.shape[0]
    heads, width, units = fast_in.shape
    weight = pl.BlockSpec((1, width, units), lambda t, s: (1 - s[0] if far else s[0], 0, 0))
    rows = pl.BlockSpec((tokens, width), lambda t, s: (0, 1 - s[0] if far else s[0]))
    copies = 1 if far else 2
    return pl.pallas_call(
        functools.partial(grad_kernel, far),
        out_shape=[jax.ShapeDtypeStruct((2, units, width), BF16), jax.ShapeDtypeStruct((width, units), BF16)] * copies,
        grid_spec=pltpu.PrefetchScalarGridSpec(
            num_scalar_prefetch=1,
            grid=(1,),
            in_specs=[rows, rows, pl.BlockSpec((heads, tokens), lambda t, h: (0, 0)), weight, weight, weight],
            out_specs=[
                pl.BlockSpec((2, units, width), lambda t, h: (0, 0, 0)),
                pl.BlockSpec((width, units), lambda t, h: (0, 0)),
            ]
            * copies,
            scratch_shapes=[pltpu.VMEM((2 * units, width), BF16), pltpu.VMEM((3 * units, tokens), BF16)],
        ),
        compiler_params=PARAMS,
        cost_estimate=pl.CostEstimate(
            flops=tokens * width * units, bytes_accessed=4 * tokens * width, transcendentals=0
        ),
        name="grads",
    )(spot, key_rows, value_rows, learn_rates, fast_in, fast_gate, fast_out)


def taken(refs, counts):
    groups, at = [], 0
    for c in counts:
        groups.append(refs[at : at + c])
        at += c
    return groups


def query_kernel(counts, masks, final, spot_ref, *refs):
    *groups, rest = taken(refs, (*counts, len(refs) - sum(counts)))
    q_refs, proj_refs, weight_refs = groups[0], groups[1], groups[2:6]
    extra_ref, *outs, normed_ref, pair_scratch, out_scratch, proj_scratch, q_scratch, tail_scratch, sems = rest
    block, lanes = normed_ref.shape
    width = lanes // 2
    step = pl.program_id(0)
    upper, rank = spot_ref[1], spot_ref[2]

    def lined(start, count):
        return pl.ds(pl.multiple_of(start, count), count)

    copies = {}

    def plan(name, source, target):
        number = sum(len(c) for c in copies.values())
        copies.setdefault(name, []).append(pltpu.make_async_copy(source, target, sems.at[number]))

    at = 0
    for ref in q_refs:
        count = min(ref.shape[0], q_scratch.shape[0] - at)
        plan("q", ref.at[pl.ds(0, count)], q_scratch.at[pl.ds(at, count)])
        at += count
    if final:
        plan("q", q_refs[-1].at[pl.ds(q_refs[-1].shape[0] - 16, 16)], tail_scratch)
    for j in range(2):
        pairs = [r.at[s] for r in weight_refs[2 * j] for s in range(r.shape[0])]
        results = [r.at[s] for r in weight_refs[2 * j + 1] for s in range(r.shape[0])]
        sides, (ranks, _, piece, _) = len(pairs), pairs[0].shape
        for s in range(sides):
            for r in range(ranks):
                start = (upper ^ s) * (ranks * piece) + (rank ^ r) * piece
                plan(j, pairs[s].at[r], pair_scratch.at[j, :, lined(start, piece), :])
                start = (rank ^ r) * (sides * piece) + (upper ^ s) * piece
                plan(j, results[r].at[s], out_scratch.at[j, lined(start, piece), :])
    rows = proj_refs[0].shape[2]
    for ref, mask in zip(proj_refs, masks):
        for k, m in enumerate(mask):
            for j in range(2):
                target = proj_scratch.at[lined((spot_ref[3] ^ m) * rows, rows), pl.ds(j * width, width)]
                plan("proj", ref.at[k, j], target)

    @pl.when(step == 0)
    def _():
        for name in ("q", 0, 1, "proj"):
            for copy in copies[name]:
                copy.start()

    def arrived(*names):
        @pl.when(step == 0)
        def _():
            for name in names:
                for copy in copies[name]:
                    copy.wait()

    arrived("q", 0, 1)
    if final:
        tail = tail_scratch[...].astype(F32)
        gains = tail[0:1] + tail[1:2] + tail[2:3]
    else:
        gains = extra_ref[...].reshape(1, lanes)
    units = out_scratch.shape[2]
    count = block // 2
    tasks = [(lo, j) for lo in range(0, block, count) for j in range(2)]
    heads = (spot_ref[0], 1 - spot_ref[0])
    columns = [pl.ds(pl.multiple_of(h * width, 128), width) for h in heads]
    both, head_out = {}, {}
    for i in range(len(tasks) + 2):
        if i < len(tasks):
            lo, j = tasks[i]
            q = q_scratch[lined(step * block + lo, count), columns[j]]
            both[i] = dot_nt(q, pair_scratch[j].reshape(-1, width))
        if 0 <= i - 1 < len(tasks):
            q_in, q_gate = both[i - 1][:, :units], both[i - 1][:, units:]
            hidden = (q_in * sigmoid(q_in) * q_gate).astype(BF16)
            head_out[i - 1] = dot_nt(hidden, out_scratch[tasks[i - 1][1]])
        if i >= 2:
            (lo, j), result = tasks[i - 2], head_out[i - 2]
            inverse = lax.rsqrt(jnp.mean(result * result, axis=-1, keepdims=True) + EPS)
            gain = jnp.where(heads[j] == 0, gains[:, :width], gains[:, width:])
            normed_ref[lo : lo + count, columns[j]] = (result * inverse * gain).astype(BF16)
    arrived("proj")
    total = dot_nt(normed_ref[...], proj_scratch[...])
    if final:
        total = total + extra_ref[...]
    else:
        outs[1][0] = pair_scratch[step, 0].T
        outs[2][0] = pair_scratch[step, 1].T
        outs[3][0] = out_scratch[step].T
    outs[0][...] = total.astype(outs[0].dtype)


def query_heads(spot, queries, gain, proj, masks, mine, theirs, earlier):
    final = earlier is not None
    tokens = sum(q.shape[0] for q in queries) - 16 * final
    lanes = queries[0].shape[1]
    width = units = lanes // 2
    outs = sum(len(m) for m in masks) * proj[0].shape[2]
    block = tokens // 2
    groups = (queries, proj, *mine, *theirs)
    counts = tuple(len(g) for g in groups)
    operands = [a for g in groups for a in g]
    in_specs = [pl.BlockSpec(memory_space=pl.ANY)] * len(operands)
    rows_spec = pl.BlockSpec((block, outs), lambda t, s: (t, 0))
    out_shape, out_specs = [jax.ShapeDtypeStruct((tokens, outs), BF16 if final else F32)], [rows_spec]
    if final:
        in_specs.append(rows_spec)
    else:
        in_specs.append(pl.BlockSpec(gain.shape, lambda t, s: (0,)))
        out_shape += [jax.ShapeDtypeStruct((2, width, units), BF16)] * 3
        out_specs += [pl.BlockSpec((1, width, units), lambda t, s: (t + s[0] - 2 * t * s[0], 0, 0))] * 3
    operands.append(earlier if final else gain)
    sides = sum(a.shape[0] for a in mine[0])
    ranks = sum(a.shape[0] for a in mine[1])
    copies = len(queries) + 1 + 4 * sides * ranks + 2 * sum(len(m) for m in masks)
    result = pl.pallas_call(
        functools.partial(query_kernel, counts, masks, final),
        out_shape=out_shape,
        grid_spec=pltpu.PrefetchScalarGridSpec(
            num_scalar_prefetch=1,
            grid=(tokens // block,),
            in_specs=in_specs,
            out_specs=out_specs,
            scratch_shapes=[
                pltpu.VMEM((block, lanes), BF16),
                pltpu.VMEM((2, 2, units, width), BF16),
                pltpu.VMEM((2, width, units), BF16),
                pltpu.VMEM((outs, lanes), BF16),
                pltpu.VMEM((tokens, lanes), BF16),
                pltpu.VMEM((16, lanes), BF16),
                pltpu.SemaphoreType.DMA((copies,)),
            ],
        ),
        compiler_params=PARAMS,
        cost_estimate=pl.CostEstimate(
            flops=12 * tokens * width * width + 4 * tokens * width * outs,
            bytes_accessed=4 * tokens * width + 12 * width * width + 4 * tokens * outs,
            transcendentals=0,
        ),
        name="queries",
    )(spot, *operands)
    return result[0] if final else result


def renorm(wide, grad):
    moved = wide - grad
    scale = jnp.sqrt(jnp.sum(wide * wide, axis=-1, keepdims=True) + EPS) / jnp.sqrt(
        jnp.sum(moved * moved, axis=-1, keepdims=True) + EPS
    )
    return (moved * scale).astype(BF16)


def on_device(n_ctx, n_head, key_rows, value_rows, query_rows, learn_rates, fast_in, fast_gate, fast_out, head_gain, out_proj):
    heads, width, units = fast_in.shape
    place = lax.axis_index("ctx")
    group = lax.axis_index("head")
    core, upper, rank = place % 2, (place // 2) % 2, place // 4
    ranks = n_ctx // 4
    half = units // 2
    piece = half // ranks

    def across(array, mask):
        return lax.ppermute(array, "ctx", [(j, j ^ mask) for j in range(n_ctx)])

    def over(array):
        return lax.ppermute(array, "head", [(j, j ^ 1) for j in range(n_head)])

    def part(array, start, count, axis=0):
        return lax.dynamic_slice_in_dim(array, start, count, axis)

    def joined(array, rider):
        flat = array.reshape(-1, width)
        return flat if rider is None else jnp.concatenate([flat, rider])

    def parted(array, like, rider):
        count = like.size // width
        return array[:count].reshape(like.shape), None if rider is None else array[count:]

    def to_upper(array_for, rider=None):
        array = array_for(1 - upper)
        return parted(across(joined(array, rider), 2), array, rider)

    def to_ranks(array_for, rider=None):
        sent = [array_for(rank ^ d) for d in range(1, ranks)]
        first, rider = parted(across(joined(sent[0], rider), 4), sent[0], rider)
        return [first] + [across(a, 4 * d) for d, a in enumerate(sent[1:], 2)], rider

    tie = lax.optimization_barrier
    inputs = (key_rows, value_rows, learn_rates, fast_in, fast_gate, fast_out)

    half_ctx = n_ctx // 2
    rows = out_proj.shape[1]
    stepwise = ranks == 4 and rows % 16 == 0
    tiled = piece % 16 == 0
    spot = [core, upper, rank] if tiled else [core, 0, 0]
    spot = jnp.stack(spot + [place % half_ctx if stepwise else 0]).astype(jnp.int32)

    tokens = query_rows.shape[0]
    third = tokens // 3 // 16 * 16
    cuts = (0, tokens - 2 * third, tokens - third, tokens)
    query_parts = [query_rows[a:b] for a, b in zip(cuts, cuts[1:])]
    far_parts = [over(query_parts[0])]
    high = lax.reduce_precision(head_gain, 8, 7)
    middle = lax.reduce_precision(head_gain - high, 8, 7)
    gain_rows = jnp.stack([high, middle, head_gain - high - middle]).astype(BF16)
    gain_rows = jnp.pad(gain_rows, ((0, 13), (0, 0)))

    here = (place // half_ctx) == group
    block = out_proj.T.reshape(rows, 2, width).transpose(1, 0, 2).reshape(2 * rows, width)
    if stepwise:
        blocks = [block, across(block, 4), across(block, 8)]
    else:
        pairs = []
        for j in range(half_ctx):
            low, high = (j * n_head) + 1, (j + half_ctx) * n_head
            pairs += [(low, high), (high, low)]
        swapped = lax.ppermute(out_proj.T, ("ctx", "head"), pairs)
        proj = lax.all_gather(jnp.where(here, out_proj.T, swapped), "ctx", axis=0, tiled=True)
        proj = proj.reshape(2, -1, 2, width).transpose(0, 2, 1, 3)
        blocks = []

    other = grads_of(spot, 1, *inputs)
    other, inputs, spot = tie((other, inputs, spot))
    got_pair, got_out = (across(a, 1) for a in other)
    own_pair, own_out, pair_old, out_old = grads_of(spot, 0, *inputs)
    own_pair, own_out, blocks, far_parts, query_parts = tie((own_pair, own_out, blocks, far_parts, query_parts))
    far_parts.append(over(query_parts[1]))

    def pair_sum(start, count):
        return part(own_pair, start, count, 1).astype(F32) + part(got_pair, start, count, 1).astype(F32)

    def out_sum(start, count):
        return part(own_out, start, count).astype(F32) + part(got_out, start, count).astype(F32)

    pair_got, _ = to_upper(lambda u: pair_sum(u * half, half).astype(BF16))
    out_got, rider = to_ranks(
        lambda r: out_sum(r * 2 * piece, 2 * piece).astype(BF16), blocks[2] if stepwise else None
    )
    pair_total = pair_sum(upper * half, half) + pair_got.astype(F32)
    out_total = out_sum(rank * 2 * piece, 2 * piece)
    for a in out_got:
        out_total = out_total + a.astype(F32)
    pair_sent, out_sent = pair_total.astype(BF16), out_total.astype(BF16)
    kept = given = None
    if stepwise:
        near, away = jnp.concatenate(blocks[:2]), jnp.concatenate([blocks[2], rider])
        kept, given = jnp.where(here, near, away), jnp.where(here, away, near)
    pair_sent, out_sent, kept, given, far_parts = tie((pair_sent, out_sent, kept, given, far_parts))
    pair_got, _ = to_ranks(lambda r: part(pair_sent, r * piece, piece, 1))
    out_got, kept_upper = to_upper(lambda u: part(out_sent, u * piece, piece), kept)
    come = over(given) if stepwise else None
    pair_grad = part(pair_total, rank * piece, piece, 1)
    for a in pair_got:
        pair_grad = pair_grad + a.astype(F32)
    out_grad = part(out_total, upper * piece, piece) + out_got.astype(F32)
    pair_wide = part(pair_old, upper * half + rank * piece, piece, 1).astype(F32)
    out_wide = part(out_old, rank * 2 * piece + upper * piece, piece).astype(F32)
    pair_new, out_new = renorm(pair_wide, pair_grad), renorm(out_wide, out_grad)
    pair_new, out_new, come, query_parts, kept, kept_upper = tie((pair_new, out_new, come, query_parts, kept, kept_upper))

    pair_got, _ = to_ranks(lambda r: pair_new)
    out_got, come_upper = to_upper(lambda u: out_new, come)
    far_parts.append(over(jnp.concatenate([query_parts[2], gain_rows])))
    far_new = over(out_new)
    pair_held, out_held = jnp.stack([pair_new] + pair_got), jnp.stack([out_new, out_got])
    if stepwise:
        masks = [[0, 4, 2, 6], [1, 5, 3, 7]]
        own_proj = [jnp.concatenate([kept, kept_upper])]
        own_proj.append(across(own_proj[0], 1))
    else:
        masks = [[0]]
        own_proj, far_proj = [part(proj, group, 1)], [part(proj, 1 - group, 1)]
    pair_held, out_held, far_parts, far_new = tie((pair_held, out_held, far_parts, far_new))

    def finish(pair, out, beside, rider=None):
        (pair_got, rider), (out_got, _) = to_upper(lambda u: pair, rider), to_ranks(lambda r: out)
        pair_got, out_got, rider, done = tie((pair_got, out_got, rider, beside()))
        return ([pair[None], pair_got[None]], [a[None] for a in (out, *out_got)]), rider, done

    mine, rider, far_pair = finish(pair_held, out_held, lambda: over(pair_held), far_new)
    far_out = jnp.stack([far_new, rider])
    mine = tuple([jnp.concatenate(g)] for g in mine)

    def settled(pair, out):
        if not tiled:
            side, order = jnp.arange(2) ^ upper, jnp.arange(ranks) ^ rank
            pair, out = jnp.concatenate(pair), jnp.concatenate(out)
            pair = jnp.take(jnp.take(pair, side, 0), order, 1).transpose(2, 0, 1, 3, 4).reshape(1, 1, 2, units, width)
            out = jnp.take(jnp.take(out, order, 0), side, 1).reshape(1, 1, units, width)
            pair, out = [pair], [out]
        return pair, out

    def swapped_cores(arrays):
        return [across(a, 1) for a in arrays]

    theirs = tuple(swapped_cores(g) for g in mine)
    mine, theirs, come, come_upper = tie((mine, theirs, come, come_upper))
    if stepwise:
        far_proj = [jnp.concatenate([come, come_upper])]
        far_proj.append(across(far_proj[0], 1))

    def blocks_of(arrays):
        return [a.reshape(-1, 2, rows, width) for a in arrays] if stepwise else arrays

    far_mine, _, ((partial, *news), far_proj) = finish(
        far_pair,
        far_out,
        lambda: (
            query_heads(
                spot, [query_rows], head_gain, blocks_of(own_proj), masks, settled(*mine), settled(*theirs), None
            ),
            far_proj,
        ),
    )
    far_theirs = tuple(swapped_cores(g) for g in far_mine)
    output = query_heads(
        spot, far_parts, None, blocks_of(far_proj), masks, settled(*far_mine), settled(*far_theirs), partial
    )
    return (output, *news)


def solution(mesh):
    return jax.shard_map(
        functools.partial(on_device, mesh.shape["ctx"], mesh.shape["head"]),
        mesh=mesh,
        in_specs=(
            P("ctx", "head"),
            P("ctx", "head"),
            P("ctx", "head"),
            P("head", "ctx"),
            P("head", None, None),
            P("head", None, None),
            P("head", None, None),
            P("head"),
            P("head", "ctx"),
        ),
        out_specs=(
            P("ctx", "head"),
            P("head", None, None),
            P("head", None, None),
            P("head", None, None),
        ),
        check_vma=False,
    )
```

```python
import functools

import jax
import jax.numpy as jnp
from jax import lax
from jax.experimental import pallas as pl
from jax.experimental.pallas import tpu as pltpu
from jax.sharding import PartitionSpec as P

F32 = jnp.float32
BF16 = jnp.bfloat16
NT = (((1,), (1,)), ((), ()))
EPS = 1e-06
VMEM_BYTES = 56 * 1024 * 1024
PARAMS = pltpu.CompilerParams(vmem_limit_bytes=VMEM_BYTES, dimension_semantics=("arbitrary",))


def dot(a, b):
    return jnp.dot(a, b, preferred_element_type=F32)


def dot_nt(a, b):
    return lax.dot_general(a, b, NT, preferred_element_type=F32)


def sigmoid(x):
    return 0.5 * jnp.tanh(0.5 * x) + 0.5


def grad_kernel(far, spot_ref, k_ref, v_ref, lr_ref, win_ref, wgate_ref, wout_ref, pair_ref, out_ref, *refs):
    w_t, backs = refs[-2:]
    units = wout_ref.shape[1]
    w_t[0:units] = win_ref[0].T
    w_t[units:] = wgate_ref[0].T
    if len(refs) > 2:
        refs[0][...] = w_t[...].reshape(refs[0].shape)
        refs[1][...] = wout_ref[0].T
    k = k_ref[...]
    v = v_ref[...]
    rate = -lr_ref[pl.ds(1 - spot_ref[0] if far else spot_ref[0], 1), :]
    count = units // 2
    for lo in range(0, units, count):
        pre_in = dot_nt(w_t[lo : lo + count], k)
        pre_gate = dot_nt(w_t[units + lo : units + lo + count], k)
        back = dot_nt(wout_ref[0, lo : lo + count], v) * rate
        sig = sigmoid(pre_in)
        act = pre_in * sig
        backs[lo : lo + count] = (back * pre_gate * (sig + act * (1.0 - sig))).astype(BF16)
        backs[units + lo : units + lo + count] = (back * act).astype(BF16)
        backs[2 * units + lo : 2 * units + lo + count] = (act * pre_gate * rate).astype(BF16)
    pair_ref[...] = dot(backs[0 : 2 * units], k).astype(BF16).reshape(pair_ref.shape)
    out_ref[...] = dot(backs[2 * units :], v).T.astype(BF16)


def grads_of(spot, far, key_rows, value_rows, learn_rates, fast_in, fast_gate, fast_out):
    tokens = key_rows.shape[0]
    heads, width, units = fast_in.shape
    weight = pl.BlockSpec((1, width, units), lambda t, s: (1 - s[0] if far else s[0], 0, 0))
    rows = pl.BlockSpec((tokens, width), lambda t, s: (0, 1 - s[0] if far else s[0]))
    copies = 1 if far else 2
    return pl.pallas_call(
        functools.partial(grad_kernel, far),
        out_shape=[jax.ShapeDtypeStruct((2, units, width), BF16), jax.ShapeDtypeStruct((width, units), BF16)] * copies,
        grid_spec=pltpu.PrefetchScalarGridSpec(
            num_scalar_prefetch=1,
            grid=(1,),
            in_specs=[rows, rows, pl.BlockSpec((heads, tokens), lambda t, h: (0, 0)), weight, weight, weight],
            out_specs=[
                pl.BlockSpec((2, units, width), lambda t, h: (0, 0, 0)),
                pl.BlockSpec((width, units), lambda t, h: (0, 0)),
            ]
            * copies,
            scratch_shapes=[pltpu.VMEM((2 * units, width), BF16), pltpu.VMEM((3 * units, tokens), BF16)],
        ),
        compiler_params=PARAMS,
        cost_estimate=pl.CostEstimate(
            flops=tokens * width * units, bytes_accessed=4 * tokens * width, transcendentals=0
        ),
        name="grads",
    )(spot, key_rows, value_rows, learn_rates, fast_in, fast_gate, fast_out)


def taken(refs, counts):
    groups, at = [], 0
    for c in counts:
        groups.append(refs[at : at + c])
        at += c
    return groups


def query_kernel(counts, masks, final, spot_ref, *refs):
    *groups, rest = taken(refs, (*counts, len(refs) - sum(counts)))
    q_refs, proj_refs, weight_refs = groups[0], groups[1], groups[2:6]
    extra_ref, *outs, normed_ref, pair_scratch, out_scratch, proj_scratch, q_scratch, tail_scratch, sems = rest
    block, lanes = normed_ref.shape
    width = lanes // 2
    step = pl.program_id(0)
    upper, rank = spot_ref[1], spot_ref[2]

    def lined(start, count):
        return pl.ds(pl.multiple_of(start, count), count)

    copies = {}

    def plan(name, source, target):
        number = sum(len(c) for c in copies.values())
        copies.setdefault(name, []).append(pltpu.make_async_copy(source, target, sems.at[number]))

    at = 0
    for ref in q_refs:
        count = min(ref.shape[0], q_scratch.shape[0] - at)
        plan("q", ref.at[pl.ds(0, count)], q_scratch.at[pl.ds(at, count)])
        at += count
    if final:
        plan("q", q_refs[-1].at[pl.ds(q_refs[-1].shape[0] - 16, 16)], tail_scratch)
    for j in range(2):
        pairs = [r.at[s] for r in weight_refs[2 * j] for s in range(r.shape[0])]
        results = [r.at[s] for r in weight_refs[2 * j + 1] for s in range(r.shape[0])]
        sides, (ranks, _, piece, _) = len(pairs), pairs[0].shape
        for s in range(sides):
            for r in range(ranks):
                start = (upper ^ s) * (ranks * piece) + (rank ^ r) * piece
                plan(j, pairs[s].at[r], pair_scratch.at[j, :, lined(start, piece), :])
                start = (rank ^ r) * (sides * piece) + (upper ^ s) * piece
                plan(j, results[r].at[s], out_scratch.at[j, lined(start, piece), :])
    rows = proj_refs[0].shape[2]
    for ref, mask in zip(proj_refs, masks):
        for k, m in enumerate(mask):
            for j in range(2):
                target = proj_scratch.at[lined((spot_ref[3] ^ m) * rows, rows), pl.ds(j * width, width)]
                plan("proj", ref.at[k, j], target)

    @pl.when(step == 0)
    def _():
        for name in ("q", 0, 1, "proj"):
            for copy in copies[name]:
                copy.start()

    def arrived(*names):
        @pl.when(step == 0)
        def _():
            for name in names:
                for copy in copies[name]:
                    copy.wait()

    arrived("q", 0, 1)
    if final:
        tail = tail_scratch[...].astype(F32)
        gains = tail[0:1] + tail[1:2] + tail[2:3]
    else:
        gains = extra_ref[...].reshape(1, lanes)
    units = out_scratch.shape[2]
    count = block // 2
    tasks = [(lo, j) for lo in range(0, block, count) for j in range(2)]
    heads = (spot_ref[0], 1 - spot_ref[0])
    columns = [pl.ds(pl.multiple_of(h * width, 128), width) for h in heads]
    both, head_out = {}, {}
    for i in range(len(tasks) + 2):
        if i < len(tasks):
            lo, j = tasks[i]
            q = q_scratch[lined(step * block + lo, count), columns[j]]
            both[i] = dot_nt(q, pair_scratch[j].reshape(-1, width))
        if 0 <= i - 1 < len(tasks):
            q_in, q_gate = both[i - 1][:, :units], both[i - 1][:, units:]
            hidden = (q_in * sigmoid(q_in) * q_gate).astype(BF16)
            head_out[i - 1] = dot_nt(hidden, out_scratch[tasks[i - 1][1]])
        if i >= 2:
            (lo, j), result = tasks[i - 2], head_out[i - 2]
            inverse = lax.rsqrt(jnp.mean(result * result, axis=-1, keepdims=True) + EPS)
            gain = jnp.where(heads[j] == 0, gains[:, :width], gains[:, width:])
            normed_ref[lo : lo + count, columns[j]] = (result * inverse * gain).astype(BF16)
    arrived("proj")
    total = dot_nt(normed_ref[...], proj_scratch[...])
    if final:
        total = total + extra_ref[...]
    else:
        outs[1][0] = pair_scratch[step, 0].T
        outs[2][0] = pair_scratch[step, 1].T
        outs[3][0] = out_scratch[step].T
    outs[0][...] = total.astype(outs[0].dtype)


def query_heads(spot, queries, gain, proj, masks, mine, theirs, earlier):
    final = earlier is not None
    tokens = sum(q.shape[0] for q in queries) - 16 * final
    lanes = queries[0].shape[1]
    width = units = lanes // 2
    outs = sum(len(m) for m in masks) * proj[0].shape[2]
    block = tokens // 2
    groups = (queries, proj, *mine, *theirs)
    counts = tuple(len(g) for g in groups)
    operands = [a for g in groups for a in g]
    in_specs = [pl.BlockSpec(memory_space=pl.ANY)] * len(operands)
    rows_spec = pl.BlockSpec((block, outs), lambda t, s: (t, 0))
    out_shape, out_specs = [jax.ShapeDtypeStruct((tokens, outs), BF16 if final else F32)], [rows_spec]
    if final:
        in_specs.append(rows_spec)
    else:
        in_specs.append(pl.BlockSpec(gain.shape, lambda t, s: (0,)))
        out_shape += [jax.ShapeDtypeStruct((2, width, units), BF16)] * 3
        out_specs += [pl.BlockSpec((1, width, units), lambda t, s: (t + s[0] - 2 * t * s[0], 0, 0))] * 3
    operands.append(earlier if final else gain)
    sides = sum(a.shape[0] for a in mine[0])
    ranks = sum(a.shape[0] for a in mine[1])
    copies = len(queries) + 1 + 4 * sides * ranks + 2 * sum(len(m) for m in masks)
    result = pl.pallas_call(
        functools.partial(query_kernel, counts, masks, final),
        out_shape=out_shape,
        grid_spec=pltpu.PrefetchScalarGridSpec(
            num_scalar_prefetch=1,
            grid=(tokens // block,),
            in_specs=in_specs,
            out_specs=out_specs,
            scratch_shapes=[
                pltpu.VMEM((block, lanes), BF16),
                pltpu.VMEM((2, 2, units, width), BF16),
                pltpu.VMEM((2, width, units), BF16),
                pltpu.VMEM((outs, lanes), BF16),
                pltpu.VMEM((tokens, lanes), BF16),
                pltpu.VMEM((16, lanes), BF16),
                pltpu.SemaphoreType.DMA((copies,)),
            ],
        ),
        compiler_params=PARAMS,
        cost_estimate=pl.CostEstimate(
            flops=12 * tokens * width * width + 4 * tokens * width * outs,
            bytes_accessed=4 * tokens * width + 12 * width * width + 4 * tokens * outs,
            transcendentals=0,
        ),
        name="queries",
    )(spot, *operands)
    return result[0] if final else result


def renorm(wide, grad):
    moved = wide - grad
    scale = jnp.sqrt(jnp.sum(wide * wide, axis=-1, keepdims=True) + EPS) / jnp.sqrt(
        jnp.sum(moved * moved, axis=-1, keepdims=True) + EPS
    )
    return (moved * scale).astype(BF16)


def on_device(n_ctx, n_head, key_rows, value_rows, query_rows, learn_rates, fast_in, fast_gate, fast_out, head_gain, out_proj):
    heads, width, units = fast_in.shape
    place = lax.axis_index("ctx")
    group = lax.axis_index("head")
    core, upper, rank = place % 2, (place // 2) % 2, place // 4
    ranks = n_ctx // 4
    half = units // 2
    piece = half // ranks

    def across(array, mask):
        return lax.ppermute(array, "ctx", [(j, j ^ mask) for j in range(n_ctx)])

    def over(array):
        return lax.ppermute(array, "head", [(j, j ^ 1) for j in range(n_head)])

    def part(array, start, count, axis=0):
        return lax.dynamic_slice_in_dim(array, start, count, axis)

    def joined(array, rider):
        flat = array.reshape(-1, width)
        return flat if rider is None else jnp.concatenate([flat, rider])

    def parted(array, like, rider):
        count = like.size // width
        return array[:count].reshape(like.shape), None if rider is None else array[count:]

    def to_upper(array_for, rider=None):
        array = array_for(1 - upper)
        return parted(across(joined(array, rider), 2), array, rider)

    def to_ranks(array_for, rider=None):
        sent = [array_for(rank ^ d) for d in range(1, ranks)]
        first, rider = parted(across(joined(sent[0], rider), 4), sent[0], rider)
        return [first] + [across(a, 4 * d) for d, a in enumerate(sent[1:], 2)], rider

    tie = lax.optimization_barrier
    inputs = (key_rows, value_rows, learn_rates, fast_in, fast_gate, fast_out)

    half_ctx = n_ctx // 2
    rows = out_proj.shape[1]
    stepwise = ranks == 4 and rows % 16 == 0
    tiled = piece % 16 == 0
    spot = [core, upper, rank] if tiled else [core, 0, 0]
    spot = jnp.stack(spot + [place % half_ctx if stepwise else 0]).astype(jnp.int32)

    tokens = query_rows.shape[0]
    third = tokens // 3 // 16 * 16
    cuts = (0, tokens - 2 * third, tokens - third, tokens)
    far_parts = [over(query_rows[cuts[0] : cuts[1]])]
    high = lax.reduce_precision(head_gain, 8, 7)
    middle = lax.reduce_precision(head_gain - high, 8, 7)
    gain_rows = jnp.stack([high, middle, head_gain - high - middle]).astype(BF16)
    gain_rows = jnp.pad(gain_rows, ((0, 13), (0, 0)))

    here = (place // half_ctx) == group
    block = out_proj.T.reshape(rows, 2, width).transpose(1, 0, 2).reshape(2 * rows, width)
    if stepwise:
        blocks = [block, across(block, 4), across(block, 8)]
    else:
        pairs = []
        for j in range(half_ctx):
            low, high = (j * n_head) + 1, (j + half_ctx) * n_head
            pairs += [(low, high), (high, low)]
        swapped = lax.ppermute(out_proj.T, ("ctx", "head"), pairs)
        proj = lax.all_gather(jnp.where(here, out_proj.T, swapped), "ctx", axis=0, tiled=True)
        proj = proj.reshape(2, -1, 2, width).transpose(0, 2, 1, 3)
        blocks = []

    other = grads_of(spot, 1, *inputs)
    other, inputs, spot = tie((other, inputs, spot))
    got_pair, got_out = (across(a, 1) for a in other)
    own_pair, own_out, pair_old, out_old = grads_of(spot, 0, *inputs)
    own_pair, own_out, blocks, far_parts, late_rows = tie((own_pair, own_out, blocks, far_parts, query_rows))

    def pair_sum(start, count):
        return part(own_pair, start, count, 1).astype(F32) + part(got_pair, start, count, 1).astype(F32)

    def out_sum(start, count):
        return part(own_out, start, count).astype(F32) + part(got_out, start, count).astype(F32)

    pair_sent, late_rows = tie((pair_sum((1 - upper) * half, half).astype(BF16), late_rows))
    pair_got, _ = to_upper(lambda u: pair_sent)
    far_parts.append(over(late_rows[cuts[1] : cuts[2]]))
    out_got, rider = to_ranks(
        lambda r: out_sum(r * 2 * piece, 2 * piece).astype(BF16), blocks[2] if stepwise else None
    )
    pair_total = pair_sum(upper * half, half) + pair_got.astype(F32)
    out_total = out_sum(rank * 2 * piece, 2 * piece)
    for a in out_got:
        out_total = out_total + a.astype(F32)
    pair_sent, out_sent = pair_total.astype(BF16), out_total.astype(BF16)
    kept = given = None
    if stepwise:
        near, away = jnp.concatenate(blocks[:2]), jnp.concatenate([blocks[2], rider])
        kept, given = jnp.where(here, near, away), jnp.where(here, away, near)
    out_sent = part(out_sent, (1 - upper) * piece, piece)
    out_joined = joined(out_sent, kept)
    pair_sent, out_joined, given, far_parts = tie((pair_sent, out_joined, given, far_parts))
    pair_got, _ = to_ranks(lambda r: part(pair_sent, r * piece, piece, 1))
    out_got, kept_upper = parted(across(out_joined, 2), out_sent, kept)
    come = over(given) if stepwise else None
    pair_grad = part(pair_total, rank * piece, piece, 1)
    for a in pair_got:
        pair_grad = pair_grad + a.astype(F32)
    out_grad = part(out_total, upper * piece, piece) + out_got.astype(F32)
    pair_wide = part(pair_old, upper * half + rank * piece, piece, 1).astype(F32)
    out_wide = part(out_old, rank * 2 * piece + upper * piece, piece).astype(F32)
    pair_new, out_new = renorm(pair_wide, pair_grad), renorm(out_wide, out_grad)
    pair_new, out_new, come, late_rows, kept, kept_upper = tie((pair_new, out_new, come, late_rows, kept, kept_upper))

    pair_got, _ = to_ranks(lambda r: pair_new)
    out_got, come_upper = to_upper(lambda u: out_new, come)
    far_parts.append(over(jnp.concatenate([late_rows[cuts[2] :], gain_rows])))
    far_new = over(out_new)
    pair_held, out_held = jnp.stack([pair_new] + pair_got), jnp.stack([out_new, out_got])
    if stepwise:
        masks = [[0, 4, 2, 6], [1, 5, 3, 7]]
        own_proj = [jnp.concatenate([kept, kept_upper])]
        own_proj.append(across(own_proj[0], 1))
    else:
        masks = [[0]]
        own_proj, far_proj = [part(proj, group, 1)], [part(proj, 1 - group, 1)]
    pair_held, out_held, far_parts, far_new = tie((pair_held, out_held, far_parts, far_new))

    def finish(pair, out, beside, rider=None):
        (pair_got, rider), (out_got, _) = to_upper(lambda u: pair, rider), to_ranks(lambda r: out)
        pair_got, out_got, rider, done = tie((pair_got, out_got, rider, beside()))
        return ([pair[None], pair_got[None]], [a[None] for a in (out, *out_got)]), rider, done

    mine, rider, far_pair = finish(pair_held, out_held, lambda: over(pair_held), far_new)
    far_out = jnp.stack([far_new, rider])
    mine = tuple([jnp.concatenate(g)] for g in mine)

    def settled(pair, out):
        if not tiled:
            side, order = jnp.arange(2) ^ upper, jnp.arange(ranks) ^ rank
            pair, out = jnp.concatenate(pair), jnp.concatenate(out)
            pair = jnp.take(jnp.take(pair, side, 0), order, 1).transpose(2, 0, 1, 3, 4).reshape(1, 1, 2, units, width)
            out = jnp.take(jnp.take(out, order, 0), side, 1).reshape(1, 1, units, width)
            pair, out = [pair], [out]
        return pair, out

    def swapped_cores(arrays):
        return [across(a, 1) for a in arrays]

    theirs = tuple(swapped_cores(g) for g in mine)
    mine, theirs, come, come_upper = tie((mine, theirs, come, come_upper))
    if stepwise:
        far_proj = [jnp.concatenate([come, come_upper])]
        far_proj.append(across(far_proj[0], 1))

    def blocks_of(arrays):
        return [a.reshape(-1, 2, rows, width) for a in arrays] if stepwise else arrays

    far_mine, _, ((partial, *news), far_proj) = finish(
        far_pair,
        far_out,
        lambda: (
            query_heads(
                spot, [query_rows], head_gain, blocks_of(own_proj), masks, settled(*mine), settled(*theirs), None
            ),
            far_proj,
        ),
    )
    far_theirs = tuple(swapped_cores(g) for g in far_mine)
    output = query_heads(
        spot, far_parts, None, blocks_of(far_proj), masks, settled(*far_mine), settled(*far_theirs), partial
    )
    return (output, *news)


def solution(mesh):
    return jax.shard_map(
        functools.partial(on_device, mesh.shape["ctx"], mesh.shape["head"]),
        mesh=mesh,
        in_specs=(
            P("ctx", "head"),
            P("ctx", "head"),
            P("ctx", "head"),
            P("head", "ctx"),
            P("head", None, None),
            P("head", None, None),
            P("head", None, None),
            P("head"),
            P("head", "ctx"),
        ),
        out_specs=(
            P("ctx", "head"),
            P("head", None, None),
            P("head", None, None),
            P("head", None, None),
        ),
        check_vma=False,
    )
```

```python
import functools

import jax
import jax.numpy as jnp
from jax import lax
from jax.experimental import pallas as pl
from jax.experimental.pallas import tpu as pltpu
from jax.sharding import PartitionSpec as P

F32 = jnp.float32
BF16 = jnp.bfloat16
NT = (((1,), (1,)), ((), ()))
EPS = 1e-06
VMEM_BYTES = 56 * 1024 * 1024
PARAMS = pltpu.CompilerParams(vmem_limit_bytes=VMEM_BYTES, dimension_semantics=("arbitrary",))


def dot(a, b):
    return jnp.dot(a, b, preferred_element_type=F32)


def dot_nt(a, b):
    return lax.dot_general(a, b, NT, preferred_element_type=F32)


def sigmoid(x):
    return 0.5 * jnp.tanh(0.5 * x) + 0.5


def grad_kernel(far, spot_ref, k_ref, v_ref, lr_ref, win_ref, wgate_ref, wout_ref, pair_ref, out_ref, *refs):
    w_t, backs = refs[-2:]
    units = wout_ref.shape[1]
    w_t[0:units] = win_ref[0].T
    w_t[units:] = wgate_ref[0].T
    if len(refs) > 2:
        refs[0][...] = w_t[...].reshape(refs[0].shape)
        refs[1][...] = wout_ref[0].T
    k = k_ref[...]
    v = v_ref[...]
    rate = -lr_ref[pl.ds(1 - spot_ref[0] if far else spot_ref[0], 1), :]
    count = units // 2
    for lo in range(0, units, count):
        pre_in = dot_nt(w_t[lo : lo + count], k)
        pre_gate = dot_nt(w_t[units + lo : units + lo + count], k)
        back = dot_nt(wout_ref[0, lo : lo + count], v) * rate
        sig = sigmoid(pre_in)
        act = pre_in * sig
        backs[lo : lo + count] = (back * pre_gate * (sig + act * (1.0 - sig))).astype(BF16)
        backs[units + lo : units + lo + count] = (back * act).astype(BF16)
        backs[2 * units + lo : 2 * units + lo + count] = (act * pre_gate * rate).astype(BF16)
    pair_ref[...] = dot(backs[0 : 2 * units], k).astype(BF16).reshape(pair_ref.shape)
    out_ref[...] = dot(backs[2 * units :], v).T.astype(BF16)


def grads_of(spot, far, key_rows, value_rows, learn_rates, fast_in, fast_gate, fast_out):
    tokens = key_rows.shape[0]
    heads, width, units = fast_in.shape
    weight = pl.BlockSpec((1, width, units), lambda t, s: (1 - s[0] if far else s[0], 0, 0))
    rows = pl.BlockSpec((tokens, width), lambda t, s: (0, 1 - s[0] if far else s[0]))
    copies = 1 if far else 2
    return pl.pallas_call(
        functools.partial(grad_kernel, far),
        out_shape=[jax.ShapeDtypeStruct((2, units, width), BF16), jax.ShapeDtypeStruct((width, units), BF16)] * copies,
        grid_spec=pltpu.PrefetchScalarGridSpec(
            num_scalar_prefetch=1,
            grid=(1,),
            in_specs=[rows, rows, pl.BlockSpec((heads, tokens), lambda t, h: (0, 0)), weight, weight, weight],
            out_specs=[
                pl.BlockSpec((2, units, width), lambda t, h: (0, 0, 0)),
                pl.BlockSpec((width, units), lambda t, h: (0, 0)),
            ]
            * copies,
            scratch_shapes=[pltpu.VMEM((2 * units, width), BF16), pltpu.VMEM((3 * units, tokens), BF16)],
        ),
        compiler_params=PARAMS,
        cost_estimate=pl.CostEstimate(
            flops=tokens * width * units, bytes_accessed=4 * tokens * width, transcendentals=0
        ),
        name="grads",
    )(spot, key_rows, value_rows, learn_rates, fast_in, fast_gate, fast_out)


def taken(refs, counts):
    groups, at = [], 0
    for c in counts:
        groups.append(refs[at : at + c])
        at += c
    return groups


def query_kernel(counts, masks, final, spot_ref, *refs):
    *groups, rest = taken(refs, (*counts, len(refs) - sum(counts)))
    q_refs, proj_refs, weight_refs = groups[0], groups[1], groups[2:6]
    extra_ref, *outs, normed_ref, pair_scratch, out_scratch, proj_scratch, q_scratch, tail_scratch, sems = rest
    block, lanes = normed_ref.shape
    width = lanes // 2
    step = pl.program_id(0)
    upper, rank = spot_ref[1], spot_ref[2]

    def lined(start, count):
        return pl.ds(pl.multiple_of(start, count), count)

    copies = {}

    def plan(name, source, target):
        number = sum(len(c) for c in copies.values())
        copies.setdefault(name, []).append(pltpu.make_async_copy(source, target, sems.at[number]))

    at = 0
    for ref in q_refs:
        count = min(ref.shape[0], q_scratch.shape[0] - at)
        plan("q", ref.at[pl.ds(0, count)], q_scratch.at[pl.ds(at, count)])
        at += count
    if final:
        plan("q", q_refs[-1].at[pl.ds(q_refs[-1].shape[0] - 16, 16)], tail_scratch)
    for j in range(2):
        pairs = [r.at[s] for r in weight_refs[2 * j] for s in range(r.shape[0])]
        results = [r.at[s] for r in weight_refs[2 * j + 1] for s in range(r.shape[0])]
        sides, (ranks, _, piece, _) = len(pairs), pairs[0].shape
        for s in range(sides):
            for r in range(ranks):
                start = (upper ^ s) * (ranks * piece) + (rank ^ r) * piece
                plan(j, pairs[s].at[r], pair_scratch.at[j, :, lined(start, piece), :])
                start = (rank ^ r) * (sides * piece) + (upper ^ s) * piece
                plan(j, results[r].at[s], out_scratch.at[j, lined(start, piece), :])
    rows = proj_refs[0].shape[2]
    for ref, mask in zip(proj_refs, masks):
        for k, m in enumerate(mask):
            for j in range(2):
                target = proj_scratch.at[lined((spot_ref[3] ^ m) * rows, rows), pl.ds(j * width, width)]
                plan("proj", ref.at[k, j], target)

    @pl.when(step == 0)
    def _():
        for name in ("q", 0, 1, "proj"):
            for copy in copies[name]:
                copy.start()

    def arrived(*names):
        @pl.when(step == 0)
        def _():
            for name in names:
                for copy in copies[name]:
                    copy.wait()

    arrived("q", 0, 1)
    if final:
        tail = tail_scratch[...].astype(F32)
        gains = tail[0:1] + tail[1:2] + tail[2:3]
    else:
        gains = extra_ref[...].reshape(1, lanes)
    units = out_scratch.shape[2]
    count = block // 2
    tasks = [(lo, j) for lo in range(0, block, count) for j in range(2)]
    heads = (spot_ref[0], 1 - spot_ref[0])
    columns = [pl.ds(pl.multiple_of(h * width, 128), width) for h in heads]
    both, head_out = {}, {}
    for i in range(len(tasks) + 2):
        if i < len(tasks):
            lo, j = tasks[i]
            q = q_scratch[lined(step * block + lo, count), columns[j]]
            both[i] = dot_nt(q, pair_scratch[j].reshape(-1, width))
        if 0 <= i - 1 < len(tasks):
            q_in, q_gate = both[i - 1][:, :units], both[i - 1][:, units:]
            hidden = (q_in * sigmoid(q_in) * q_gate).astype(BF16)
            head_out[i - 1] = dot_nt(hidden, out_scratch[tasks[i - 1][1]])
        if i >= 2:
            (lo, j), result = tasks[i - 2], head_out[i - 2]
            inverse = lax.rsqrt(jnp.mean(result * result, axis=-1, keepdims=True) + EPS)
            gain = jnp.where(heads[j] == 0, gains[:, :width], gains[:, width:])
            normed_ref[lo : lo + count, columns[j]] = (result * inverse * gain).astype(BF16)
    arrived("proj")
    total = dot_nt(normed_ref[...], proj_scratch[...])
    if final:
        total = total + extra_ref[...]
    else:
        outs[1][0] = pair_scratch[step, 0].T
        outs[2][0] = pair_scratch[step, 1].T
        outs[3][0] = out_scratch[step].T
    outs[0][...] = total.astype(outs[0].dtype)


def query_heads(spot, queries, gain, proj, masks, mine, theirs, earlier):
    final = earlier is not None
    tokens = sum(q.shape[0] for q in queries) - 16 * final
    lanes = queries[0].shape[1]
    width = units = lanes // 2
    outs = sum(len(m) for m in masks) * proj[0].shape[2]
    block = tokens // 2
    groups = (queries, proj, *mine, *theirs)
    counts = tuple(len(g) for g in groups)
    operands = [a for g in groups for a in g]
    in_specs = [pl.BlockSpec(memory_space=pl.ANY)] * len(operands)
    rows_spec = pl.BlockSpec((block, outs), lambda t, s: (t, 0))
    out_shape, out_specs = [jax.ShapeDtypeStruct((tokens, outs), BF16 if final else F32)], [rows_spec]
    if final:
        in_specs.append(rows_spec)
    else:
        in_specs.append(pl.BlockSpec(gain.shape, lambda t, s: (0,)))
        out_shape += [jax.ShapeDtypeStruct((2, width, units), BF16)] * 3
        out_specs += [pl.BlockSpec((1, width, units), lambda t, s: (t + s[0] - 2 * t * s[0], 0, 0))] * 3
    operands.append(earlier if final else gain)
    sides = sum(a.shape[0] for a in mine[0])
    ranks = sum(a.shape[0] for a in mine[1])
    copies = len(queries) + 1 + 4 * sides * ranks + 2 * sum(len(m) for m in masks)
    result = pl.pallas_call(
        functools.partial(query_kernel, counts, masks, final),
        out_shape=out_shape,
        grid_spec=pltpu.PrefetchScalarGridSpec(
            num_scalar_prefetch=1,
            grid=(tokens // block,),
            in_specs=in_specs,
            out_specs=out_specs,
            scratch_shapes=[
                pltpu.VMEM((block, lanes), BF16),
                pltpu.VMEM((2, 2, units, width), BF16),
                pltpu.VMEM((2, width, units), BF16),
                pltpu.VMEM((outs, lanes), BF16),
                pltpu.VMEM((tokens, lanes), BF16),
                pltpu.VMEM((16, lanes), BF16),
                pltpu.SemaphoreType.DMA((copies,)),
            ],
        ),
        compiler_params=PARAMS,
        cost_estimate=pl.CostEstimate(
            flops=12 * tokens * width * width + 4 * tokens * width * outs,
            bytes_accessed=4 * tokens * width + 12 * width * width + 4 * tokens * outs,
            transcendentals=0,
        ),
        name="queries",
    )(spot, *operands)
    return result[0] if final else result


def renorm(wide, grad):
    moved = wide - grad
    scale = jnp.sqrt(jnp.sum(wide * wide, axis=-1, keepdims=True) + EPS) / jnp.sqrt(
        jnp.sum(moved * moved, axis=-1, keepdims=True) + EPS
    )
    return (moved * scale).astype(BF16)


def on_device(n_ctx, n_head, key_rows, value_rows, query_rows, learn_rates, fast_in, fast_gate, fast_out, head_gain, out_proj):
    heads, width, units = fast_in.shape
    place = lax.axis_index("ctx")
    group = lax.axis_index("head")
    core, upper, rank = place % 2, (place // 2) % 2, place // 4
    ranks = n_ctx // 4
    half = units // 2
    piece = half // ranks

    def across(array, mask):
        return lax.ppermute(array, "ctx", [(j, j ^ mask) for j in range(n_ctx)])

    def over(array):
        return lax.ppermute(array, "head", [(j, j ^ 1) for j in range(n_head)])

    def part(array, start, count, axis=0):
        return lax.dynamic_slice_in_dim(array, start, count, axis)

    def joined(array, rider):
        flat = array.reshape(-1, width)
        return flat if rider is None else jnp.concatenate([flat, rider])

    def parted(array, like, rider):
        count = like.size // width
        return array[:count].reshape(like.shape), None if rider is None else array[count:]

    def to_upper(array_for, rider=None):
        array = array_for(1 - upper)
        return parted(across(joined(array, rider), 2), array, rider)

    def to_ranks(array_for, rider=None):
        sent = [array_for(rank ^ d) for d in range(1, ranks)]
        first, rider = parted(across(joined(sent[0], rider), 4), sent[0], rider)
        return [first] + [across(a, 4 * d) for d, a in enumerate(sent[1:], 2)], rider

    tie = lax.optimization_barrier
    inputs = (key_rows, value_rows, learn_rates, fast_in, fast_gate, fast_out)

    half_ctx = n_ctx // 2
    rows = out_proj.shape[1]
    stepwise = ranks == 4 and rows % 16 == 0
    tiled = piece % 16 == 0
    spot = [core, upper, rank] if tiled else [core, 0, 0]
    spot = jnp.stack(spot + [place % half_ctx if stepwise else 0]).astype(jnp.int32)

    tokens = query_rows.shape[0]
    third = tokens // 3 // 16 * 16
    cuts = (0, tokens - 2 * third, tokens - third, tokens)
    far_parts = [over(query_rows[cuts[0] : cuts[1]])]
    high = lax.reduce_precision(head_gain, 8, 7)
    middle = lax.reduce_precision(head_gain - high, 8, 7)
    gain_rows = jnp.stack([high, middle, head_gain - high - middle]).astype(BF16)
    gain_rows = jnp.pad(gain_rows, ((0, 13), (0, 0)))

    here = (place // half_ctx) == group
    block = out_proj.T.reshape(rows, 2, width).transpose(1, 0, 2).reshape(2 * rows, width)
    if stepwise:
        blocks = [block, across(block, 4), across(block, 8)]
    else:
        pairs = []
        for j in range(half_ctx):
            low, high = (j * n_head) + 1, (j + half_ctx) * n_head
            pairs += [(low, high), (high, low)]
        swapped = lax.ppermute(out_proj.T, ("ctx", "head"), pairs)
        proj = lax.all_gather(jnp.where(here, out_proj.T, swapped), "ctx", axis=0, tiled=True)
        proj = proj.reshape(2, -1, 2, width).transpose(0, 2, 1, 3)
        blocks = []

    other = grads_of(spot, 1, *inputs)
    other, inputs, spot = tie((other, inputs, spot))
    got_pair, got_out = (across(a, 1) for a in other)
    own_pair, own_out, pair_old, out_old = grads_of(spot, 0, *inputs)
    own_pair, own_out, blocks, far_parts, late_rows = tie((own_pair, own_out, blocks, far_parts, query_rows))

    def pair_sum(start, count):
        return part(own_pair, start, count, 1).astype(F32) + part(got_pair, start, count, 1).astype(F32)

    def out_sum(start, count):
        return part(own_out, start, count).astype(F32) + part(got_out, start, count).astype(F32)

    pair_sent, late_rows = tie((pair_sum((1 - upper) * half, half).astype(BF16), late_rows))
    pair_got, _ = to_upper(lambda u: pair_sent)
    far_parts.append(over(late_rows[cuts[1] : cuts[2]]))
    out_got, rider = to_ranks(
        lambda r: out_sum(r * 2 * piece, 2 * piece).astype(BF16), blocks[2] if stepwise else None
    )
    pair_total = pair_sum(upper * half, half) + pair_got.astype(F32)
    out_total = out_sum(rank * 2 * piece, 2 * piece)
    for a in out_got:
        out_total = out_total + a.astype(F32)
    pair_sent, out_sent = pair_total.astype(BF16), out_total.astype(BF16)
    kept = given = None
    if stepwise:
        near, away = jnp.concatenate(blocks[:2]), jnp.concatenate([blocks[2], rider])
        kept, given = jnp.where(here, near, away), jnp.where(here, away, near)
    pair_sent, out_sent, kept, given, far_parts = tie((pair_sent, out_sent, kept, given, far_parts))
    pair_got, _ = to_ranks(lambda r: part(pair_sent, r * piece, piece, 1))
    out_got, kept_upper = to_upper(lambda u: part(out_sent, u * piece, piece), kept)
    come = over(given) if stepwise else None
    out_grad = part(out_total, upper * piece, piece) + out_got.astype(F32)
    pair_wide = part(pair_old, upper * half + rank * piece, piece, 1).astype(F32)
    out_wide = part(out_old, rank * 2 * piece + upper * piece, piece).astype(F32)
    out_new = renorm(out_wide, out_grad)
    out_new, pair_got = tie((out_new, pair_got))
    pair_grad = part(pair_total, rank * piece, piece, 1)
    for a in pair_got:
        pair_grad = pair_grad + a.astype(F32)
    pair_new = renorm(pair_wide, pair_grad)
    pair_new, out_new, come, late_rows, kept, kept_upper = tie((pair_new, out_new, come, late_rows, kept, kept_upper))

    pair_got, _ = to_ranks(lambda r: pair_new)
    out_got, come_upper = to_upper(lambda u: out_new, come)
    far_parts.append(over(jnp.concatenate([late_rows[cuts[2] :], gain_rows])))
    far_new = over(out_new)
    pair_held, out_held = jnp.stack([pair_new] + pair_got), jnp.stack([out_new, out_got])
    if stepwise:
        masks = [[0, 4, 2, 6], [1, 5, 3, 7]]
        own_proj = [jnp.concatenate([kept, kept_upper])]
        own_proj.append(across(own_proj[0], 1))
    else:
        masks = [[0]]
        own_proj, far_proj = [part(proj, group, 1)], [part(proj, 1 - group, 1)]
    pair_held, out_held, far_parts, far_new = tie((pair_held, out_held, far_parts, far_new))

    def finish(pair, out, beside, rider=None):
        (pair_got, rider), (out_got, _) = to_upper(lambda u: pair, rider), to_ranks(lambda r: out)
        pair_got, out_got, rider, done = tie((pair_got, out_got, rider, beside()))
        return ([pair[None], pair_got[None]], [a[None] for a in (out, *out_got)]), rider, done

    mine, rider, far_pair = finish(pair_held, out_held, lambda: over(pair_held), far_new)
    far_out = jnp.stack([far_new, rider])
    mine = tuple([jnp.concatenate(g)] for g in mine)

    def settled(pair, out):
        if not tiled:
            side, order = jnp.arange(2) ^ upper, jnp.arange(ranks) ^ rank
            pair, out = jnp.concatenate(pair), jnp.concatenate(out)
            pair = jnp.take(jnp.take(pair, side, 0), order, 1).transpose(2, 0, 1, 3, 4).reshape(1, 1, 2, units, width)
            out = jnp.take(jnp.take(out, order, 0), side, 1).reshape(1, 1, units, width)
            pair, out = [pair], [out]
        return pair, out

    def swapped_cores(arrays):
        return [across(a, 1) for a in arrays]

    theirs = tuple(swapped_cores(g) for g in mine)
    mine, theirs, come, come_upper = tie((mine, theirs, come, come_upper))
    if stepwise:
        far_proj = [jnp.concatenate([come, come_upper])]
        far_proj.append(across(far_proj[0], 1))

    def blocks_of(arrays):
        return [a.reshape(-1, 2, rows, width) for a in arrays] if stepwise else arrays

    far_mine, _, ((partial, *news), far_proj) = finish(
        far_pair,
        far_out,
        lambda: (
            query_heads(
                spot, [query_rows], head_gain, blocks_of(own_proj), masks, settled(*mine), settled(*theirs), None
            ),
            far_proj,
        ),
    )
    far_theirs = tuple(swapped_cores(g) for g in far_mine)
    output = query_heads(
        spot, far_parts, None, blocks_of(far_proj), masks, settled(*far_mine), settled(*far_theirs), partial
    )
    return (output, *news)


def solution(mesh):
    return jax.shard_map(
        functools.partial(on_device, mesh.shape["ctx"], mesh.shape["head"]),
        mesh=mesh,
        in_specs=(
            P("ctx", "head"),
            P("ctx", "head"),
            P("ctx", "head"),
            P("head", "ctx"),
            P("head", None, None),
            P("head", None, None),
            P("head", None, None),
            P("head"),
            P("head", "ctx"),
        ),
        out_specs=(
            P("ctx", "head"),
            P("head", None, None),
            P("head", None, None),
            P("head", None, None),
        ),
        check_vma=False,
    )
```
